32 devices in a mesh: dp: 8 (over z, y), tensor: 4 (over x, core).
Axes of the slice: x: 2, y: 2, z: 4, core: 2. Of those that a mesh axis runs over, the one named last changes fastest.
Arguments:
- hidden_in: bfloat16 [8, 512, 4096], P('dp', None, 'tensor'), may hold values from -6 to 6
- norm_gain: bfloat16 [4096], replicated, may hold values from 0.25 to 1.75
- w_query: bfloat16 [4096, 4096], P('dp', 'tensor'), may hold values from -0.09375 to 0.09375
- w_key: bfloat16 [4096, 1024], P('dp', 'tensor'), may hold values from -0.09375 to 0.09375
- w_value: bfloat16 [4096, 1024], P('dp', 'tensor'), may hold values from -0.09375 to 0.09375
- w_out: bfloat16 [4096, 4096], P('tensor', 'dp'), may hold values from -0.09375 to 0.09375
- final_gain: bfloat16 [4096], P('tensor'), may hold values from 0.25 to 1.75
- latents: bfloat16 [512, 4096], P(None, 'tensor'), may hold values from -200 to 200
- token_mask: int32 [8, 512], P('dp'), may hold values from 0 to 1, as said below
- queries: bfloat16 [16384, 4096], P('dp', 'tensor'), may hold values from -6 to 6
Outputs:
- similarity_matrix: float32 [16384, 8], P('dp')
- log_norm: float32 [16384], P('dp')
The draws below stay inside these ranges and needn't reach their ends.
Inputs may be any that keep to these rules, and one draw needn't show every extreme that they name: `token_mask`: in each passage the mask is 1 on a leading run of at least 64 tokens and 0 after it; the first passage has no padding.
All inputs are finite; a program needn't handle non-finite values.
Results may differ from the reference program's by a relative error of at most 0.015.
Values may be sent and summed in bfloat16 or wider, within the bound.
A program may use at most 128 MiB of HBM per device.

```python
import jax
import jax.numpy as jnp
from jax import lax

D = 4096
HEADS = 32
KV_HEADS = 8
HEAD = 128
LATENTS = 512
LEN = 512
PASSAGES = 8
QUERIES = 16384


def draw_latents(key, part):
    key = jax.random.fold_in(key, 7)
    base = jax.random.normal(key, (LATENTS, D), jnp.float32)
    base = jnp.clip(base, -6.0, 6.0)
    return base.astype(jnp.bfloat16)


def draw_token_mask(key, part):
    key = jax.random.fold_in(key, 3)
    lengths = jax.random.randint(key, (PASSAGES, 1), LEN // 8, LEN + 1)
    lengths = lengths.at[0, 0].set(LEN)
    sequence_indices = jnp.arange(LEN, dtype=jnp.int32)[None, :]
    return (sequence_indices < lengths).astype(jnp.int32)


def steps_of(own_key, extent, shards, smallest, top_value):
    gain, own = 1.0, jax.random.fold_in(own_key, 6)
    for dim, parts in shards:
        steps = jnp.exp(jax.random.uniform(jax.random.fold_in(own, dim), (parts,), jnp.float32, smallest / len(shards), top_value / len(shards)))
        gain = gain * jnp.repeat(steps, extent[dim] // parts).reshape([-1 if axis == dim else 1 for axis in range(len(extent))])
    return gain


def bell_draw(own_key, shape, spread, bound, pieces=(), kind=jnp.bfloat16):
    drawn = jax.random.normal(own_key, shape, jnp.float32) * spread
    if len(pieces) > 0:
        drawn = steps_of(own_key, shape, pieces, -0.22, 0.18) * drawn
    return jnp.clip(drawn, min=-bound, max=bound).astype(kind)


def setup_inputs(seed: int = 0) -> dict:
    arg_keys = jax.random.split(jax.random.key(seed), 11)
    return {
        "hidden_in": bell_draw(arg_keys[0], (PASSAGES, LEN, D), 1.0, 6.0, ((0, 8), (2, 4))),
        "norm_gain": jnp.clip(1.0 + 0.15 * jax.random.normal(arg_keys[1], (D,), jnp.float32), 0.25, 1.75).astype(jnp.bfloat16),
        "w_query": bell_draw(arg_keys[2], (D, D), D ** -0.5, 0.09375, ((0, 8), (1, 4))),
        "w_key": bell_draw(arg_keys[3], (D, KV_HEADS * HEAD), D ** -0.5, 0.09375, ((0, 8), (1, 4))),
        "w_value": bell_draw(arg_keys[4], (D, KV_HEADS * HEAD), D ** -0.5, 0.09375, ((0, 8), (1, 4))),
        "w_out": bell_draw(arg_keys[5], (D, D), D ** -0.5, 0.09375, ((0, 4), (1, 8))),
        "final_gain": jnp.clip(1.0 + 0.15 * jax.random.normal(arg_keys[6], (D,), jnp.float32), 0.25, 1.75).astype(jnp.bfloat16),
        "latents": draw_latents(jax.random.fold_in(arg_keys[10], 71), 0),
        "token_mask": draw_token_mask(jax.random.fold_in(arg_keys[10], 71), 0),
        "queries": bell_draw(arg_keys[9], (QUERIES, D), 1.0, 6.0, ((0, 8), (1, 4))),
    }


EPS = 1e-05
logit_divisor = 0.02

def apply_rotary(values, sequence_indices):
    half = values.shape[-1] // 2
    freqs = 10000.0 ** (-2.0 * jnp.arange(half, dtype=jnp.float32) / values.shape[-1])
    angle = sequence_indices[:, None] * freqs[None, :]
    cosine = jnp.cos(angle)[:, None, :]
    sine = jnp.sin(angle)[:, None, :]
    first = values[..., :half]
    second = values[..., half:]
    return jnp.concatenate([first * cosine - second * sine, second * cosine + first * sine], axis=-1)

def reference(hidden_in, norm_gain, w_query, w_key, w_value, w_out, final_gain, latents, token_mask, queries):
    group = HEADS // KV_HEADS
    scale = HEAD ** (-0.5)
    sequence_indices = jnp.arange(LEN, dtype=jnp.float32)
    lat_f = latents.astype(jnp.float32).reshape(LATENTS, HEADS, HEAD)

    def one(pair):
        tokens, mask = pair
        full_f = tokens.astype(jnp.float32)
        normed = (full_f * lax.rsqrt(lax.optimization_barrier(jnp.mean(full_f * full_f, -1, keepdims=True)) + EPS) * norm_gain.astype(jnp.float32)).astype(jnp.bfloat16)
        query = jnp.dot(normed, w_query, preferred_element_type=jnp.float32)
        key = jnp.dot(normed, w_key, preferred_element_type=jnp.float32)
        value = jnp.dot(normed, w_value, preferred_element_type=jnp.float32)
        q_rot = apply_rotary(query.reshape(LEN, HEADS, HEAD), sequence_indices).astype(jnp.bfloat16).reshape(LEN, KV_HEADS, group, HEAD)
        k_rot = apply_rotary(key.reshape(LEN, KV_HEADS, HEAD), sequence_indices).astype(jnp.bfloat16)
        v_half = value.astype(jnp.bfloat16).reshape(LEN, KV_HEADS, HEAD)
        logits = jnp.einsum('qgrd,kgd->grqk', q_rot.astype(jnp.float32), k_rot.astype(jnp.float32)) * scale
        logits = jnp.where(mask[None, None, None, :] > 0, logits, -1e+30)
        attention_weights = jax.nn.softmax(logits, axis=-1).astype(jnp.bfloat16)
        attended_values = jnp.einsum('grqk,kgd->qgrd', attention_weights.astype(jnp.float32), v_half.astype(jnp.float32))
        attended_values = attended_values.astype(jnp.bfloat16).reshape(LEN, D)
        h_new = (full_f + jnp.dot(attended_values, w_out, preferred_element_type=jnp.float32)).astype(jnp.bfloat16)
        h_f = h_new.astype(jnp.float32)
        hn = (h_f * lax.rsqrt(lax.optimization_barrier(jnp.mean(h_f * h_f, -1, keepdims=True)) + EPS) * final_gain.astype(jnp.float32)).astype(jnp.bfloat16)
        hn_f = hn.astype(jnp.float32)
        cross_logits = jnp.einsum('qhd,khd->hqk', hn_f.reshape(LEN, HEADS, HEAD), lat_f) * scale
        latent_cross_weights = jax.nn.softmax(cross_logits, axis=-1).astype(jnp.bfloat16)
        cross = jnp.einsum('hqk,khd->qhd', latent_cross_weights.astype(jnp.float32), lat_f).reshape(LEN, D)
        mask_f = mask.astype(jnp.float32)
        summed = lax.optimization_barrier(jnp.sum((hn_f + cross) * mask_f[:, None], axis=0))
        return summed / jnp.sum(mask_f)
    pooled = lax.map(one, (hidden_in, token_mask))
    embedding = (pooled * lax.rsqrt(lax.optimization_barrier(jnp.sum(pooled * pooled, -1, keepdims=True)) + 1e-06)).astype(jnp.bfloat16)
    inner_product_matrix = jnp.dot(queries, embedding.T, preferred_element_type=jnp.float32)
    q_f = queries.astype(jnp.float32)
    question_norm_sq = lax.optimization_barrier(jnp.sum(q_f * q_f, -1))
    similarity_matrix = inner_product_matrix * lax.rsqrt(question_norm_sq + 1e-06)[:, None] / logit_divisor
    log_norm = jax.nn.logsumexp(similarity_matrix, axis=1)
    return (similarity_matrix, log_norm)
```

```python
import functools

import jax
import jax.numpy as jnp
from jax import lax
from jax.experimental import pallas as pl
from jax.experimental.pallas import tpu as pltpu
from jax.sharding import PartitionSpec as P

HEAD = 128
EPS = 1e-05
logit_divisor = 0.02
MESH = pl.DeviceIdType.MESH
NT_DIMS = (((1,), (1,)), ((), ()))


def layer_kernel(
    ndp, nt,
    hid_ref, mask_ref, wp_ref, wo_ref, gain_ref, cos_ref, sin_ref,
    h_ref,
    hidb, maskb, wbuf, wob, acc, atts, att, rss, rsr, hsum,
    hsend, hrecv, msem, ysend, wsend, wrecv, asem, osend, orecv, rsend, rrecv,
):
    nz = ndp // 2
    nb = ndp // nt
    length, cw = hid_ref.shape
    _, rows, pack = wp_ref.shape
    half_q = att.shape[2]
    heads = half_q // HEAD
    d_model = cw * nt
    me = lax.axis_index("dp")
    t = lax.axis_index("tensor")
    zi = me // 2
    y = lax.rem(me, 2)
    oy = 1 - y
    nbr = 2 * zi + oy
    left = me - 2
    right = me + 2
    core_t = t + 1 - 2 * lax.rem(t, 2)
    x_t = lax.rem(t + 2, nt)
    has_left = zi > 0
    has_right = zi < nz - 1

    def rcopy(src, dst, ss, rs, dpi, ti):
        return pltpu.make_async_remote_copy(
            src_ref=src, dst_ref=dst, send_sem=ss, recv_sem=rs,
            device_id=(dpi, ti), device_id_type=MESH,
        )

    barrier = pltpu.get_barrier_semaphore()
    pl.semaphore_signal(barrier, inc=1, device_id=(nbr, t), device_id_type=MESH)
    for d in range(1, nt):
        pl.semaphore_signal(
            barrier, inc=1, device_id=(me, lax.rem(t + d, nt)), device_id_type=MESH
        )

    @pl.when(has_left)
    def _():
        pl.semaphore_signal(barrier, inc=1, device_id=(left, t), device_id_type=MESH)

    @pl.when(has_right)
    def _():
        pl.semaphore_signal(barrier, inc=1, device_id=(right, t), device_id_type=MESH)

    pl.semaphore_wait(
        barrier, nt + has_left.astype(jnp.int32) + has_right.astype(jnp.int32)
    )

    def w_copy(direction, slot, p, src):
        target = right if direction == 0 else left
        return rcopy(
            src, wbuf.at[slot, p], wsend.at[direction, slot, p], wrecv.at[slot, p], target, t
        )

    def w_wait(slot, p):
        rcopy(
            wbuf.at[slot, p], wbuf.at[slot, p], ysend, wrecv.at[slot, p], nbr, t
        ).wait_recv()

    def w_send(slot, p, src):
        @pl.when(has_right)
        def _():
            w_copy(0, slot, p, src).start()

        @pl.when(has_left)
        def _():
            w_copy(1, slot, p, src).start()

    def h_copy(src, a, b, i, dpi, ti):
        return rcopy(src, hidb.at[a, b], hsend.at[i], hrecv.at[a, b], dpi, ti)

    def h_wait(a, b):
        h_copy(hidb.at[a, b], a, b, 0, nbr, t).wait_recv()

    y_copy = rcopy(wp_ref.at[oy], wbuf.at[zi, y], ysend, wrecv.at[zi, y], nbr, t)
    m_copy = rcopy(mask_ref, maskb.at[y], msem.at[0], msem.at[1], nbr, t)
    sends = [
        h_copy(hid_ref, y, t, 0, nbr, t),
        h_copy(hid_ref, y, t, 1, me, x_t),
        h_copy(hid_ref, y, t, 2, me, core_t),
        h_copy(hidb.at[oy, t], oy, t, 3, me, x_t),
        h_copy(hidb.at[oy, t], oy, t, 4, me, core_t),
        h_copy(hidb.at[y, x_t], y, x_t, 5, me, core_t),
        h_copy(hidb.at[oy, x_t], oy, x_t, 6, me, core_t),
    ]
    y_copy.start()
    w_send(zi, y, wp_ref.at[y])
    sends[0].start()
    sends[1].start()
    sends[2].start()
    m_copy.start()

    hidb[y, t] = hid_ref[...]
    maskb[y] = mask_ref[...]
    wbuf[zi, y] = wp_ref[y]
    wob[me] = wo_ref[...]
    acc[...] = jnp.zeros_like(acc)

    w_wait(zi, oy)
    w_send(zi, oy, wbuf.at[zi, oy])

    h_wait(oy, t)
    sends[3].start()
    sends[4].start()
    h_wait(y, x_t)
    sends[5].start()

    def o_copy(kind, z, src):
        target = (right, left, nbr)[kind]
        slot = 2 * z + y
        return rcopy(src, wob.at[slot], osend.at[kind, z], orecv.at[slot], target, t)

    o_copy(2, zi, wo_ref).start()

    def forward(s):
        lo = zi - s
        hi = zi + s

        @pl.when(lo >= 0)
        def _():
            for p in range(2):
                w_wait(lo, p)

                @pl.when(has_right)
                def _():
                    w_copy(0, lo, p, wbuf.at[lo, p]).start()

        @pl.when(hi < nz)
        def _():
            for p in range(2):
                w_wait(hi, p)

                @pl.when(has_left)
                def _():
                    w_copy(1, hi, p, wbuf.at[hi, p]).start()

    tile = 256

    def multiply(slot):
        for p in range(2):
            first = (slot * 2 + p) * rows
            block = first // cw
            off = pl.multiple_of(lax.rem(first, cw), 128)

            def step(i, carry):
                b = i // (length // tile)
                r = pl.multiple_of(lax.rem(i, length // tile) * tile, tile)
                acc[b, pl.ds(r, tile), :] += jnp.dot(
                    hidb[b, block, pl.ds(r, tile), pl.ds(off, rows)],
                    wbuf[slot, p],
                    preferred_element_type=jnp.float32,
                )
                return carry

            lax.fori_loop(0, 2 * (length // tile), step, 0)

    def multiply_pair(s):
        @pl.when(zi - s >= 0)
        def _():
            multiply(zi - s)

        @pl.when(zi + s < nz)
        def _():
            multiply(zi + s)

    forward(1)
    h_wait(oy, x_t)
    sends[6].start()
    for a, b in ((y, core_t), (oy, core_t)):
        h_wait(a, b)
    x_core = lax.rem(core_t + 2, nt)
    for a, b in ((y, x_core), (oy, x_core)):
        h_wait(a, b)
    for copy in sends:
        copy.wait_send()

    norm_rows = 64

    def normalise(i, carry):
        b = i // (length // norm_rows)
        r = pl.multiple_of(lax.rem(i, length // norm_rows) * norm_rows, norm_rows)
        total = jnp.zeros((norm_rows, 1), jnp.float32)
        for k in range(nt):
            x = hidb[b, k, pl.ds(r, norm_rows), :].astype(jnp.float32)
            total += jnp.sum(x * x, axis=-1, keepdims=True)
        factor = lax.rsqrt(total / d_model + EPS)
        for k in range(nt):
            x = hidb[b, k, pl.ds(r, norm_rows), :].astype(jnp.float32)
            g = gain_ref[:, k * cw : (k + 1) * cw].astype(jnp.float32)
            hidb[b, k, pl.ds(r, norm_rows), :] = (x * factor * g).astype(jnp.bfloat16)
        return carry

    lax.fori_loop(0, 2 * (length // norm_rows), normalise, 0)

    multiply(zi)
    multiply_pair(1)

    def later(s, carry):
        forward(s)
        multiply_pair(s)
        return carry

    lax.fori_loop(2, nz, later, 0)

    def o_send(z, src):
        @pl.when(has_right)
        def _():
            o_copy(0, z, src).start()

        @pl.when(has_left)
        def _():
            o_copy(1, z, src).start()

    o_send(zi, wo_ref)
    m_copy.wait()

    def rotate(x):
        return (x * cos_ref[...] + pltpu.roll(x, HEAD // 2, 1) * sin_ref[...]).astype(
            jnp.bfloat16
        )

    def attend(b, out):
        key = rotate(acc[b, :, half_q : half_q + HEAD])
        val = acc[b, :, half_q + HEAD : half_q + 2 * HEAD].astype(jnp.bfloat16)
        keep = maskb[b][0:1, :] > 0
        for j in range(heads):
            qr = rotate(acc[b, :, j * HEAD : (j + 1) * HEAD])
            logits = lax.dot_general(qr, key, NT_DIMS, preferred_element_type=jnp.float32)
            logits = jnp.where(keep, logits * HEAD**-0.5, -1e30)
            e = jnp.exp(logits - jnp.max(logits, axis=-1, keepdims=True))
            w = (e * (1.0 / jnp.sum(e, axis=-1, keepdims=True))).astype(jnp.bfloat16)
            o = jnp.dot(w, val, preferred_element_type=jnp.float32).astype(jnp.bfloat16)
            out[:, j * HEAD : (j + 1) * HEAD] = o

    attend(oy, atts)
    a_copy = rcopy(atts, att.at[y], asem.at[0], asem.at[1], nbr, t)
    a_copy.start()
    attend(y, att.at[y])
    a_copy.wait()

    def r_copy(c):
        owner = c // nb
        d = lax.rem(owner - t + nt, nt)
        return rcopy(
            rss.at[c], rsr.at[d - 1, lax.rem(c, nb)], rsend.at[c],
            rrecv.at[d - 1, lax.rem(c, nb)], me, owner,
        )

    def project(c):
        mine = c // nb == t

        def step(i, carry):
            r = pl.multiple_of(i * tile, tile)
            term = jnp.dot(
                att[0, pl.ds(r, tile), :], wob[c, 0:half_q, :],
                preferred_element_type=jnp.float32,
            ) + jnp.dot(
                att[1, pl.ds(r, tile), :], wob[c, half_q : 2 * half_q, :],
                preferred_element_type=jnp.float32,
            )

            @pl.when(mine)
            def _():
                hsum[lax.rem(c, nb), pl.ds(r, tile), :] = term

            @pl.when(jnp.logical_not(mine))
            def _():
                rss[c, pl.ds(r, tile), :] = term.astype(jnp.bfloat16)

            return carry

        lax.fori_loop(0, length // tile, step, 0)

        @pl.when(jnp.logical_not(mine))
        def _():
            r_copy(c).start()

    def other(z):
        @pl.when((z >= 0) & (z < nz))
        def _():
            slot = 2 * z + oy
            rcopy(
                wob.at[slot], wob.at[slot], osend.at[2, z], orecv.at[slot], nbr, t
            ).wait_recv()
            project(slot)

    def o_step(s, carry):
        lo = zi - s
        hi = zi + s

        @pl.when(lo >= 0)
        def _():
            slot = wob.at[2 * lo + y]
            o_copy(2, lo, slot).wait_recv()

            @pl.when(has_right)
            def _():
                o_copy(0, lo, slot).start()

            o_copy(2, lo, slot).start()

        @pl.when(hi < nz)
        def _():
            slot = wob.at[2 * hi + y]
            o_copy(2, hi, slot).wait_recv()

            @pl.when(has_left)
            def _():
                o_copy(1, hi, slot).start()

            o_copy(2, hi, slot).start()

        @pl.when(lo >= 0)
        def _():
            project(2 * lo + y)

        @pl.when(hi < nz)
        def _():
            project(2 * hi + y)

        @pl.when(s >= 2)
        def _():
            other(zi - s + 1)
            other(zi + s - 1)

        return carry

    project(me)
    other(zi)
    lax.fori_loop(1, nz, o_step, 0)
    other(zi - nz + 1)
    other(zi + nz - 1)

    for cb in range(nb):
        cols = slice(cb * rows, (cb + 1) * rows)
        for d in range(1, nt):
            rcopy(
                rss.at[0], rsr.at[d - 1, cb], rsend.at[0], rrecv.at[d - 1, cb], me,
                lax.rem(t + d, nt),
            ).wait_recv()
        total = hsum[cb]
        for d in range(1, nt):
            total += rsr[d - 1, cb].astype(jnp.float32)
        h_ref[:, cols] = (hid_ref[:, cols].astype(jnp.float32) + total).astype(jnp.bfloat16)

    y_copy.wait_send()

    def drain(z, carry):
        o_copy(2, z, wob.at[2 * z + y]).wait_send()

        @pl.when(has_right & (z <= zi))
        def _():
            o_copy(0, z, wob.at[2 * z + y]).wait_send()
            for p in range(2):
                w_copy(0, z, p, wbuf.at[z, p]).wait_send()

        @pl.when(has_left & (z >= zi))
        def _():
            o_copy(1, z, wob.at[2 * z + y]).wait_send()
            for p in range(2):
                w_copy(1, z, p, wbuf.at[z, p]).wait_send()

        return carry

    lax.fori_loop(0, nz, drain, 0)

    def drain_terms(c, carry):
        @pl.when(c // nb != t)
        def _():
            r_copy(c).wait_send()

        return carry

    lax.fori_loop(0, ndp, drain_terms, 0)


def layer(ndp, nt, rows, mask, wp, wo, gain, cosine, sine):
    length, cw = rows.shape
    _, depth, pack = wp.shape
    half_q = wo.shape[0] // 2
    nz, nb = ndp // 2, ndp // nt
    dma = pltpu.SemaphoreType.DMA
    bf, f32 = jnp.bfloat16, jnp.float32
    return pl.pallas_call(
        functools.partial(layer_kernel, ndp, nt),
        out_shape=jax.ShapeDtypeStruct((length, cw), bf),
        in_specs=[pl.BlockSpec(memory_space=pltpu.VMEM)] * 7,
        out_specs=pl.BlockSpec(memory_space=pltpu.VMEM),
        scratch_shapes=[
            pltpu.VMEM((2, nt, length, cw), bf),
            pltpu.VMEM((2,) + mask.shape, mask.dtype),
            pltpu.VMEM((nz, 2, depth, pack), bf),
            pltpu.VMEM((ndp,) + wo.shape, bf),
            pltpu.VMEM((2, length, pack), f32),
            pltpu.VMEM((length, half_q), bf),
            pltpu.VMEM((2, length, half_q), bf),
            pltpu.VMEM((ndp, length, wo.shape[1]), bf),
            pltpu.VMEM((nt - 1, nb, length, wo.shape[1]), bf),
            pltpu.VMEM((nb, length, wo.shape[1]), f32),
            dma((7,)),
            dma((2, nt)),
            dma((2,)),
            dma,
            dma((2, nz, 2)),
            dma((nz, 2)),
            dma((2,)),
            dma((3, nz)),
            dma((ndp,)),
            dma((ndp,)),
            dma((nt - 1, nb)),
        ],
        compiler_params=pltpu.CompilerParams(
            collective_id=0, has_side_effects=True, vmem_limit_bytes=58 * 1024 * 1024
        ),
    )(rows, mask, wp, wo, gain, cosine, sine)


def local(
    ndp, nt,
    hidden_in, norm_gain, w_query, w_key, w_value, w_out, final_gain, latents, token_mask, queries,
):
    count_p, length, part_width = hidden_in.shape
    rows = hidden_in.reshape(length, part_width)
    width = part_width * nt
    shard_heads = part_width // HEAD
    scale = HEAD ** (-0.5)

    half = HEAD // 2
    freqs = 10000.0 ** (-2.0 * jnp.arange(half, dtype=jnp.float32) / HEAD)
    angle = jnp.arange(length, dtype=jnp.float32)[:, None] * freqs[None, :]
    cosine = jnp.concatenate([jnp.cos(angle)] * 2, axis=1)
    sine = jnp.concatenate([-jnp.sin(angle), jnp.sin(angle)], axis=1)

    def halves(w):
        return w.reshape(w.shape[0], 2, w.shape[1] // 2).transpose(1, 0, 2)

    wp = jnp.concatenate([halves(w_query), halves(w_key), halves(w_value)], axis=2)
    mask8 = jnp.broadcast_to(token_mask, (8, length))
    h = layer(ndp, nt, rows, mask8, wp, w_out, norm_gain[None, :], cosine, sine)

    h_own = h.astype(jnp.float32)
    total_sq = lax.psum(jnp.sum(h_own * h_own, -1), "tensor")[:, None]
    hn = (h_own * lax.rsqrt(total_sq / width + EPS) * final_gain.astype(jnp.float32)).astype(
        jnp.bfloat16
    )
    hn_heads = hn.reshape(count_p, length, shard_heads, HEAD)
    lat_heads = latents.reshape(latents.shape[0], shard_heads, HEAD)
    cross_logits = (
        jnp.einsum("pqhd,khd->phqk", hn_heads, lat_heads, preferred_element_type=jnp.float32)
        * scale
    )
    latent_cross_weights = jax.nn.softmax(cross_logits, axis=-1).astype(jnp.bfloat16)
    cross = jnp.einsum(
        "phqk,khd->pqhd", latent_cross_weights, lat_heads, preferred_element_type=jnp.float32
    )
    mixed = hn.astype(jnp.float32).reshape(count_p, length, part_width) + cross.reshape(
        count_p, length, part_width
    )
    mask_f = token_mask.astype(jnp.float32)
    pooled = jnp.sum(mixed * mask_f[:, :, None], axis=1) / jnp.sum(mask_f, axis=1, keepdims=True)
    pooled_sq = lax.psum(jnp.sum(pooled * pooled, -1, keepdims=True), "tensor")
    embedding = (pooled * lax.rsqrt(pooled_sq + 1e-06)).astype(jnp.bfloat16)
    every = lax.all_gather(embedding, "dp", axis=0, tiled=True)
    inner_product_matrix = lax.dot_general(
        queries, every, (((1,), (1,)), ((), ())), preferred_element_type=jnp.float32
    )
    q_f = queries.astype(jnp.float32)
    question_norm_sq = jnp.sum(q_f * q_f, -1)
    inner_product_matrix, question_norm_sq = lax.psum(
        (inner_product_matrix, question_norm_sq), "tensor"
    )
    similarity_matrix = (
        inner_product_matrix * lax.rsqrt(question_norm_sq + 1e-06)[:, None] / logit_divisor
    )
    log_norm = jax.nn.logsumexp(similarity_matrix, axis=1)
    return (similarity_matrix, log_norm)


def solution(mesh):
    placed = (
        P("dp", None, "tensor"),
        P(),
        P("dp", "tensor"),
        P("dp", "tensor"),
        P("dp", "tensor"),
        P("tensor", "dp"),
        P("tensor"),
        P(None, "tensor"),
        P("dp", None),
        P("dp", "tensor"),
    )
    return jax.shard_map(
        functools.partial(local, mesh.shape["dp"], mesh.shape["tensor"]),
        mesh=mesh, in_specs=placed, out_specs=(P("dp", None), P("dp")), check_vma=False,
    )
```

```python
import functools

import jax
import jax.numpy as jnp
import numpy as np
from jax import lax
from jax.experimental import pallas as pl
from jax.experimental.pallas import tpu as pltpu
from jax.sharding import PartitionSpec as P

HEAD = 128
EPS = 1e-05
logit_divisor = 0.02
MESH = pl.DeviceIdType.MESH
NT_DIMS = (((1,), (1,)), ((), ()))


def layer_kernel(
    ndp, nt,
    hid_ref, mask_ref, wq_ref, wk_ref, wv_ref, wo_ref, gain_ref, cos_ref, sin_ref,
    fgain_ref, lat_ref, query_ref,
    sim_ref, norm_ref,
    hidb, maskb, wp_ref, wbuf, wob, acc, atts, att, rss, rsr, hsum,
    hbuf, colb, fown, frec, qbuf, qown, qrec, prow, sown, srec,
    hsend, hrecv, msem, ysend, wsend, wrecv, asem, osend, orecv, rsend, rrecv,
    fsend, frecv, qload, qsend, qrecv, psend, precv, ssend, srecv,
):
    nz = ndp // 2
    nb = ndp // nt
    length, cw = hid_ref.shape
    rows = wq_ref.shape[0]
    half_q = att.shape[2]
    heads = half_q // HEAD
    d_model = cw * nt
    me = lax.axis_index("dp")
    t = lax.axis_index("tensor")
    zi = me // 2
    y = lax.rem(me, 2)
    oy = 1 - y
    nbr = 2 * zi + oy
    left = me - 2
    right = me + 2
    core_t = t + 1 - 2 * lax.rem(t, 2)
    x_t = lax.rem(t + 2, nt)
    has_left = zi > 0
    has_right = zi < nz - 1

    def rcopy(src, dst, ss, rs, dpi, ti):
        return pltpu.make_async_remote_copy(
            src_ref=src, dst_ref=dst, send_sem=ss, recv_sem=rs,
            device_id=(dpi, ti), device_id_type=MESH,
        )

    q_load = pltpu.make_async_copy(query_ref, qbuf, qload)
    q_load.start()

    barrier = pltpu.get_barrier_semaphore()

    def greet(d, carry):
        pl.semaphore_signal(
            barrier, inc=1, device_id=(lax.rem(me + d, ndp), t), device_id_type=MESH
        )
        return carry

    lax.fori_loop(1, ndp, greet, 0)
    for d in range(1, nt):
        pl.semaphore_signal(
            barrier, inc=1, device_id=(me, lax.rem(t + d, nt)), device_id_type=MESH
        )

    half_k = wk_ref.shape[1] // 2
    for p in range(2):
        wp_ref[p, :, 0:half_q] = wq_ref[:, p * half_q : (p + 1) * half_q]
        wp_ref[p, :, half_q : half_q + half_k] = wk_ref[:, p * half_k : (p + 1) * half_k]
        wp_ref[p, :, half_q + half_k :] = wv_ref[:, p * half_k : (p + 1) * half_k]

    pl.semaphore_wait(barrier, ndp - 1 + nt - 1)

    def w_copy(direction, slot, p, src):
        target = right if direction == 0 else left
        return rcopy(
            src, wbuf.at[slot, p], wsend.at[direction, slot, p], wrecv.at[slot, p], target, t
        )

    def w_wait(slot, p):
        rcopy(
            wbuf.at[slot, p], wbuf.at[slot, p], ysend, wrecv.at[slot, p], nbr, t
        ).wait_recv()

    def w_send(slot, p, src):
        @pl.when(has_right)
        def _():
            w_copy(0, slot, p, src).start()

        @pl.when(has_left)
        def _():
            w_copy(1, slot, p, src).start()

    def h_copy(src, a, b, i, dpi, ti):
        return rcopy(src, hidb.at[a, b], hsend.at[i], hrecv.at[a, b], dpi, ti)

    def h_wait(a, b):
        h_copy(hidb.at[a, b], a, b, 0, nbr, t).wait_recv()

    y_copy = rcopy(wp_ref.at[oy], wbuf.at[zi, y], ysend, wrecv.at[zi, y], nbr, t)
    m_copy = rcopy(mask_ref, maskb.at[y], msem.at[0], msem.at[1], nbr, t)
    sends = [
        h_copy(hid_ref, y, t, 0, nbr, t),
        h_copy(hid_ref, y, t, 1, me, x_t),
        h_copy(hid_ref, y, t, 2, me, core_t),
        h_copy(hidb.at[oy, t], oy, t, 3, me, x_t),
        h_copy(hidb.at[oy, t], oy, t, 4, me, core_t),
        h_copy(hidb.at[y, x_t], y, x_t, 5, me, core_t),
        h_copy(hidb.at[oy, x_t], oy, x_t, 6, me, core_t),
    ]
    y_copy.start()
    w_send(zi, y, wp_ref.at[y])
    sends[1].start()
    sends[2].start()

    hidb[y, t] = hid_ref[...]
    maskb[y] = mask_ref[...]
    wbuf[zi, y] = wp_ref[y]
    wob[me] = wo_ref[...]
    acc[...] = jnp.zeros_like(acc)

    w_wait(zi, oy)
    w_send(zi, oy, wbuf.at[zi, oy])
    sends[0].start()
    m_copy.start()
    h_wait(y, x_t)
    sends[5].start()

    pieces = 4
    depth = wo_ref.shape[0] // pieces

    def o_copy(kind, z, k, own=False):
        target = (right, left, nbr)[kind]
        slot = 2 * z + y
        part = pl.ds(k * depth, depth)
        src = wo_ref.at[part] if own else wob.at[slot, part]
        return rcopy(
            src, wob.at[slot, part], osend.at[kind, z, k], orecv.at[slot, k], target, t
        )

    def o_wait(slot, k):
        part = wob.at[slot, pl.ds(k * depth, depth)]
        rcopy(part, part, osend.at[2, 0, k], orecv.at[slot, k], nbr, t).wait_recv()

    def forward(s):
        lo = zi - s
        hi = zi + s

        @pl.when(lo >= 0)
        def _():
            for p in range(2):
                w_wait(lo, p)

                @pl.when(has_right)
                def _():
                    w_copy(0, lo, p, wbuf.at[lo, p]).start()

        @pl.when(hi < nz)
        def _():
            for p in range(2):
                w_wait(hi, p)

                @pl.when(has_left)
                def _():
                    w_copy(1, hi, p, wbuf.at[hi, p]).start()

    tile = 256

    def multiply(slot):
        for p in range(2):
            first = (slot * 2 + p) * rows
            block = first // cw
            off = pl.multiple_of(lax.rem(first, cw), 128)

            def step(i, carry):
                b = i // (length // tile)
                r = pl.multiple_of(lax.rem(i, length // tile) * tile, tile)
                acc[b, pl.ds(r, tile), :] += jnp.dot(
                    hidb[b, block, pl.ds(r, tile), pl.ds(off, rows)],
                    wbuf[slot, p],
                    preferred_element_type=jnp.float32,
                )
                return carry

            lax.fori_loop(0, 2 * (length // tile), step, 0)

    def multiply_pair(s):
        @pl.when(zi - s >= 0)
        def _():
            multiply(zi - s)

        @pl.when(zi + s < nz)
        def _():
            multiply(zi + s)

    forward(1)
    h_wait(oy, t)
    sends[3].start()
    sends[4].start()
    for k in range(pieces):
        o_copy(2, zi, k, own=True).start()

    ones = jnp.ones((8, cw), jnp.bfloat16)

    def row_sums(x):
        x = x.astype(jnp.float32)
        square = x * x
        high = square.astype(jnp.bfloat16)
        low = (square - high.astype(jnp.float32)).astype(jnp.bfloat16)
        return lax.dot_general(
            ones, high, NT_DIMS, preferred_element_type=jnp.float32
        ) + lax.dot_general(ones, low, NT_DIMS, preferred_element_type=jnp.float32)

    def over_tensor(d, src, dst, ss, rs):
        return rcopy(
            src, dst.at[d - 1], ss.at[d - 1], rs.at[d - 1], me, lax.rem(t + d, nt)
        )

    q_load.wait()
    count = qbuf.shape[0]

    def query_norm(i, carry):
        r = pl.multiple_of(i * 128, 128)
        qown[:, pl.ds(r, 128)] = row_sums(qbuf[pl.ds(r, 128), :])
        return carry

    lax.fori_loop(0, count // 128, query_norm, 0)
    q_copies = [over_tensor(d, qown, qrec, qsend, qrecv) for d in range(1, nt)]
    h_wait(oy, x_t)
    sends[6].start()
    for copy in q_copies:
        copy.start()
    for a, b in ((y, core_t), (oy, core_t)):
        h_wait(a, b)
    x_core = lax.rem(core_t + 2, nt)
    for a, b in ((y, x_core), (oy, x_core)):
        h_wait(a, b)
    for copy in sends:
        copy.wait_send()

    norm_rows = 64

    def normalise(i, carry):
        b = i // (length // norm_rows)
        r = pl.multiple_of(lax.rem(i, length // norm_rows) * norm_rows, norm_rows)
        total = jnp.zeros((norm_rows, 1), jnp.float32)
        for k in range(nt):
            x = hidb[b, k, pl.ds(r, norm_rows), :].astype(jnp.float32)
            total += jnp.sum(x * x, axis=-1, keepdims=True)
        factor = lax.rsqrt(total / d_model + EPS)
        for k in range(nt):
            x = hidb[b, k, pl.ds(r, norm_rows), :].astype(jnp.float32)
            g = gain_ref[:, k * cw : (k + 1) * cw].astype(jnp.float32)
            hidb[b, k, pl.ds(r, norm_rows), :] = (x * factor * g).astype(jnp.bfloat16)
        return carry

    lax.fori_loop(0, 2 * (length // norm_rows), normalise, 0)

    multiply(zi)

    def later(s, carry):
        forward(s)
        multiply_pair(s - 1)
        return carry

    lax.fori_loop(2, nz, later, 0)

    for k in range(pieces):

        @pl.when(has_right)
        def _():
            o_copy(0, zi, k, own=True).start()

        @pl.when(has_left)
        def _():
            o_copy(1, zi, k, own=True).start()

    multiply_pair(nz - 1)
    m_copy.wait()

    def rotate(x):
        return (x * cos_ref[...] + pltpu.roll(x, HEAD // 2, 1) * sin_ref[...]).astype(
            jnp.bfloat16
        )

    def attend(b, out):
        key = rotate(acc[b, :, half_q : half_q + HEAD])
        val = acc[b, :, half_q + HEAD : half_q + 2 * HEAD].astype(jnp.bfloat16)
        keep = maskb[b][0:1, :] > 0
        for j in range(heads):
            qr = rotate(acc[b, :, j * HEAD : (j + 1) * HEAD])
            logits = lax.dot_general(qr, key, NT_DIMS, preferred_element_type=jnp.float32)
            logits = jnp.where(keep, logits * HEAD**-0.5, -1e30)
            e = jnp.exp(logits - jnp.max(logits, axis=-1, keepdims=True))
            w = (e * (1.0 / jnp.sum(e, axis=-1, keepdims=True))).astype(jnp.bfloat16)
            o = jnp.dot(w, val, preferred_element_type=jnp.float32).astype(jnp.bfloat16)
            out[:, j * HEAD : (j + 1) * HEAD] = o

    attend(oy, atts)
    a_copy = rcopy(atts, att.at[y], asem.at[0], asem.at[1], nbr, t)
    a_copy.start()
    attend(y, att.at[y])
    a_copy.wait()

    def r_copy(c):
        owner = c // nb
        d = lax.rem(owner - t + nt, nt)
        return rcopy(
            rss.at[c], rsr.at[d - 1, lax.rem(c, nb)], rsend.at[c],
            rrecv.at[d - 1, lax.rem(c, nb)], me, owner,
        )

    def project(c):
        mine = c // nb == t

        def step(i, carry):
            r = pl.multiple_of(i * tile, tile)
            term = jnp.dot(
                att[0, pl.ds(r, tile), :], wob[c, 0:half_q, :],
                preferred_element_type=jnp.float32,
            ) + jnp.dot(
                att[1, pl.ds(r, tile), :], wob[c, half_q : 2 * half_q, :],
                preferred_element_type=jnp.float32,
            )

            @pl.when(mine)
            def _():
                hsum[lax.rem(c, nb), pl.ds(r, tile), :] = term

            @pl.when(jnp.logical_not(mine))
            def _():
                rss[c, pl.ds(r, tile), :] = term.astype(jnp.bfloat16)

            return carry

        lax.fori_loop(0, length // tile, step, 0)

        @pl.when(jnp.logical_not(mine))
        def _():
            r_copy(c).start()

    def other(z):
        @pl.when((z >= 0) & (z < nz))
        def _():
            slot = 2 * z + oy
            for k in range(pieces):
                o_wait(slot, k)
            project(slot)

    def o_step(s, carry):
        lo = zi - s
        hi = zi + s
        for k in range(pieces):

            @pl.when(lo >= 0)
            def _():
                o_wait(2 * lo + y, k)

                @pl.when(has_right)
                def _():
                    o_copy(0, lo, k).start()

                o_copy(2, lo, k).start()

            @pl.when(hi < nz)
            def _():
                o_wait(2 * hi + y, k)

                @pl.when(has_left)
                def _():
                    o_copy(1, hi, k).start()

                o_copy(2, hi, k).start()

        @pl.when(lo >= 0)
        def _():
            project(2 * lo + y)

        @pl.when(hi < nz)
        def _():
            project(2 * hi + y)

        @pl.when(s >= 2)
        def _():
            other(zi - s + 1)
            other(zi + s - 1)

        return carry

    project(me)
    other(zi)
    lax.fori_loop(1, nz, o_step, 0)
    other(zi - nz + 1)
    other(zi + nz - 1)

    for cb in range(nb):
        for d in range(1, nt):
            rcopy(
                rss.at[0], rsr.at[d - 1, cb], rsend.at[0], rrecv.at[d - 1, cb], me,
                lax.rem(t + d, nt),
            ).wait_recv()

    def add_terms(i, carry):
        r = pl.multiple_of(i * 128, 128)
        part = pl.ds(r, 128)
        for cb in range(nb):
            cols = slice(cb * rows, (cb + 1) * rows)
            total = hsum[cb, part, :]
            for d in range(1, nt):
                total += rsr[d - 1, cb, part, :].astype(jnp.float32)
            hbuf[part, cols] = (hid_ref[part, cols].astype(jnp.float32) + total).astype(
                jnp.bfloat16
            )
        fown[:, part] = row_sums(hbuf[part, :])
        return carry

    lax.fori_loop(0, length // 128, add_terms, 0)
    f_copies = [over_tensor(d, fown, frec, fsend, frecv) for d in range(1, nt)]
    for copy in f_copies:
        copy.start()
    mask_row = mask_ref[...].astype(jnp.float32)
    tokens = jnp.sum(mask_row[0:1, :], axis=1, keepdims=True)
    mask_col = jnp.broadcast_to(mask_row[0:1, :], (128, length)).T[:, 0:1]
    for copy in f_copies:
        copy.wait_recv()
    squares = fown[0:1, :]
    for d in range(1, nt):
        squares += frec[d - 1][0:1, :]
    factor_row = lax.rsqrt(squares / d_model + EPS)
    colb[...] = jnp.broadcast_to(factor_row, (128, length)).T

    def final_norm(i, carry):
        r = pl.multiple_of(i * norm_rows, norm_rows)
        part = pl.ds(r, norm_rows)
        x = hbuf[part, :].astype(jnp.float32)
        g = fgain_ref[...].astype(jnp.float32)
        hbuf[part, :] = (x * colb[part, 0:1] * g).astype(jnp.bfloat16)
        return carry

    lax.fori_loop(0, length // norm_rows, final_norm, 0)

    for j in range(cw // HEAD):
        cols = slice(j * HEAD, (j + 1) * HEAD)
        hn = hbuf[:, cols]
        lat = lat_ref[:, cols]
        logits = lax.dot_general(hn, lat, NT_DIMS, preferred_element_type=jnp.float32)
        logits = logits * HEAD**-0.5
        e = jnp.exp(logits - jnp.max(logits, axis=-1, keepdims=True))
        w = (e * (1.0 / jnp.sum(e, axis=-1, keepdims=True))).astype(jnp.bfloat16)
        mixed = hn.astype(jnp.float32) + jnp.dot(w, lat, preferred_element_type=jnp.float32)
        pooled = jnp.sum(mixed * mask_col, axis=0, keepdims=True) / tokens
        prow[me, :, cols] = jnp.broadcast_to(pooled, (8, HEAD))

    def p_copy(d):
        return rcopy(
            prow.at[me], prow.at[me], psend.at[d - 1], precv.at[me], lax.rem(me + d, ndp), t
        )

    def p_start(d, carry):
        p_copy(d).start()
        return carry

    def p_wait(d, carry):
        src = lax.rem(me + d, ndp)
        rcopy(
            prow.at[src], prow.at[src], psend.at[d - 1], precv.at[src], src, t
        ).wait_recv()
        return carry

    lax.fori_loop(1, ndp, p_start, 0)
    lax.fori_loop(1, ndp, p_wait, 0)
    every = jnp.concatenate([prow[i, 0:1, :] for i in range(ndp)], axis=0)
    sown[:, count:] = jnp.broadcast_to(
        jnp.sum(every * every, axis=1, keepdims=True), (ndp, 128)
    )
    every = every.astype(jnp.bfloat16)

    def score(i, carry):
        r = pl.multiple_of(i * 256, 256)
        sown[:, pl.ds(r, 256)] = lax.dot_general(
            every, qbuf[pl.ds(r, 256), :], NT_DIMS, preferred_element_type=jnp.float32
        )
        return carry

    lax.fori_loop(0, count // 256, score, 0)
    s_copies = [over_tensor(d, sown, srec, ssend, srecv) for d in range(1, nt)]
    for copy in s_copies:
        copy.start()
    for copy in q_copies + s_copies:
        copy.wait_recv()
    scores = sown[...]
    query_sq = qown[0:1, :]
    for d in range(1, nt):
        scores += srec[d - 1]
        query_sq += qrec[d - 1][0:1, :]
    similarity = (
        scores[:, :count]
        * lax.rsqrt(scores[:, count : count + 1] + 1e-06)
        * (lax.rsqrt(query_sq + 1e-06) / logit_divisor)
    )
    sim_ref[...] = similarity
    top = jnp.max(similarity, axis=0, keepdims=True)
    norm_ref[...] = top + jnp.log(jnp.sum(jnp.exp(similarity - top), axis=0, keepdims=True))

    for copy in f_copies + q_copies + s_copies:
        copy.wait_send()

    def p_drain(d, carry):
        p_copy(d).wait_send()
        return carry

    lax.fori_loop(1, ndp, p_drain, 0)

    y_copy.wait_send()

    def drain(z, carry):
        for k in range(pieces):
            o_copy(2, z, k).wait_send()

        @pl.when(has_right & (z <= zi))
        def _():
            for k in range(pieces):
                o_copy(0, z, k).wait_send()
            for p in range(2):
                w_copy(0, z, p, wbuf.at[z, p]).wait_send()

        @pl.when(has_left & (z >= zi))
        def _():
            for k in range(pieces):
                o_copy(1, z, k).wait_send()
            for p in range(2):
                w_copy(1, z, p, wbuf.at[z, p]).wait_send()

        return carry

    lax.fori_loop(0, nz, drain, 0)

    def drain_terms(c, carry):
        @pl.when(c // nb != t)
        def _():
            r_copy(c).wait_send()

        return carry

    lax.fori_loop(0, ndp, drain_terms, 0)


def layer(ndp, nt, rows, mask, wq, wk, wv, wo, gain, cosine, sine, fgain, lat, queries):
    length, cw = rows.shape
    depth = wq.shape[0]
    pack = (wq.shape[1] + wk.shape[1] + wv.shape[1]) // 2
    half_q = wo.shape[0] // 2
    nz, nb = ndp // 2, ndp // nt
    count = queries.shape[0]
    dma = pltpu.SemaphoreType.DMA
    bf, f32 = jnp.bfloat16, jnp.float32
    vmem = pl.BlockSpec(memory_space=pltpu.VMEM)
    return pl.pallas_call(
        functools.partial(layer_kernel, ndp, nt),
        out_shape=(
            jax.ShapeDtypeStruct((ndp, count), f32),
            jax.ShapeDtypeStruct((1, count), f32),
        ),
        in_specs=[vmem] * 11 + [pl.BlockSpec(memory_space=pl.ANY)],
        out_specs=(vmem, vmem),
        scratch_shapes=[
            pltpu.VMEM((2, nt, length, cw), bf),
            pltpu.VMEM((2,) + mask.shape, mask.dtype),
            pltpu.VMEM((2, depth, pack), bf),
            pltpu.VMEM((nz, 2, depth, pack), bf),
            pltpu.VMEM((ndp,) + wo.shape, bf),
            pltpu.VMEM((2, length, pack), f32),
            pltpu.VMEM((length, half_q), bf),
            pltpu.VMEM((2, length, half_q), bf),
            pltpu.VMEM((ndp, length, wo.shape[1]), bf),
            pltpu.VMEM((nt - 1, nb, length, wo.shape[1]), bf),
            pltpu.VMEM((nb, length, wo.shape[1]), f32),
            pltpu.VMEM((length, cw), bf),
            pltpu.VMEM((length, 128), f32),
            pltpu.VMEM((8, length), f32),
            pltpu.VMEM((nt - 1, 8, length), f32),
            pltpu.VMEM((count, cw), bf),
            pltpu.VMEM((8, count), f32),
            pltpu.VMEM((nt - 1, 8, count), f32),
            pltpu.VMEM((ndp, 8, cw), f32),
            pltpu.VMEM((ndp, count + 128), f32),
            pltpu.VMEM((nt - 1, ndp, count + 128), f32),
            dma((7,)),
            dma((2, nt)),
            dma((2,)),
            dma,
            dma((2, nz, 2)),
            dma((nz, 2)),
            dma((2,)),
            dma((3, nz, 4)),
            dma((ndp, 4)),
            dma((ndp,)),
            dma((nt - 1, nb)),
            dma((nt - 1,)),
            dma((nt - 1,)),
            dma,
            dma((nt - 1,)),
            dma((nt - 1,)),
            dma((ndp - 1,)),
            dma((ndp,)),
            dma((nt - 1,)),
            dma((nt - 1,)),
        ],
        compiler_params=pltpu.CompilerParams(
            collective_id=0, has_side_effects=True, vmem_limit_bytes=60 * 1024 * 1024
        ),
    )(rows, mask, wq, wk, wv, wo, gain, cosine, sine, fgain, lat, queries)


def local(
    ndp, nt,
    hidden_in, norm_gain, w_query, w_key, w_value, w_out, final_gain, latents, token_mask, queries,
):
    _, length, part_width = hidden_in.shape
    rows = hidden_in.reshape(length, part_width)
    half = HEAD // 2
    freqs = np.float32(10000.0) ** (-2.0 * np.arange(half, dtype=np.float32) / HEAD)
    angle = np.arange(length, dtype=np.float32)[:, None] * freqs.astype(np.float32)[None, :]
    cosine = jnp.asarray(np.concatenate([np.cos(angle)] * 2, axis=1), jnp.float32)
    sine = jnp.asarray(np.concatenate([-np.sin(angle), np.sin(angle)], axis=1), jnp.float32)
    mask8 = jnp.broadcast_to(token_mask, (8, length))
    similarity, log_norm = layer(
        ndp, nt, rows, mask8, w_query, w_key, w_value, w_out, norm_gain[None, :], cosine, sine,
        final_gain[None, :], latents, queries,
    )
    return similarity.T, log_norm[0]


def solution(mesh):
    placed = (
        P("dp", None, "tensor"),
        P(),
        P("dp", "tensor"),
        P("dp", "tensor"),
        P("dp", "tensor"),
        P("tensor", "dp"),
        P("tensor"),
        P(None, "tensor"),
        P("dp", None),
        P("dp", "tensor"),
    )
    return jax.shard_map(
        functools.partial(local, mesh.shape["dp"], mesh.shape["tensor"]),
        mesh=mesh, in_specs=placed, out_specs=(P("dp", None), P("dp")), check_vma=False,
    )
```

```python
import functools

import jax
import jax.numpy as jnp
import numpy as np
from jax import lax
from jax.experimental import pallas as pl
from jax.experimental.pallas import tpu as pltpu
from jax.sharding import PartitionSpec as P

HEAD = 128
EPS = 1e-05
logit_divisor = 0.02
MESH = pl.DeviceIdType.MESH
NT_DIMS = (((1,), (1,)), ((), ()))


def layer_kernel(
    ndp, nt,
    hid_ref, mask_ref, wq_ref, wk_ref, wv_ref, wo_ref, gain_ref, cos_ref, sin_ref,
    fgain_ref, lat_ref, query_ref,
    sim_ref, norm_ref,
    hidb, maskb, wp_ref, wbuf, wob, acc, atts, att, rss, rsr, hsum,
    hbuf, colb, fown, frec, qbuf, qown, qrec, prow, sown, srec,
    hsend, hrecv, msem, ysend, wsend, wrecv, asem, osend, orecv, rsend, rrecv,
    fsend, frecv, qload, qsend, qrecv, psend, precv, ssend, srecv,
):
    nz = ndp // 2
    nb = ndp // nt
    pieces, _, wide = wob.shape[1:]
    length, cw = hid_ref.shape
    rows = wq_ref.shape[0]
    half_q = att.shape[2]
    heads = half_q // HEAD
    d_model = cw * nt
    me = lax.axis_index("dp")
    t = lax.axis_index("tensor")
    zi = me // 2
    y = lax.rem(me, 2)
    oy = 1 - y
    nbr = 2 * zi + oy
    left = me - 2
    right = me + 2
    core_t = t + 1 - 2 * lax.rem(t, 2)
    x_t = lax.rem(t + 2, nt)
    has_left = zi > 0
    has_right = zi < nz - 1

    def rcopy(src, dst, ss, rs, dpi, ti):
        return pltpu.make_async_remote_copy(
            src_ref=src, dst_ref=dst, send_sem=ss, recv_sem=rs,
            device_id=(dpi, ti), device_id_type=MESH,
        )

    q_load = pltpu.make_async_copy(query_ref, qbuf, qload)
    q_load.start()

    barrier = pltpu.get_barrier_semaphore()

    def greet(d, carry):
        pl.semaphore_signal(
            barrier, inc=1, device_id=(lax.rem(me + d, ndp), t), device_id_type=MESH
        )
        return carry

    lax.fori_loop(1, ndp, greet, 0)
    for d in range(1, nt):
        pl.semaphore_signal(
            barrier, inc=1, device_id=(me, lax.rem(t + d, nt)), device_id_type=MESH
        )

    half_k = wk_ref.shape[1] // 2
    for p in range(2):
        wp_ref[p, :, 0:half_q] = wq_ref[:, p * half_q : (p + 1) * half_q]
        wp_ref[p, :, half_q : half_q + half_k] = wk_ref[:, p * half_k : (p + 1) * half_k]
        wp_ref[p, :, half_q + half_k :] = wv_ref[:, p * half_k : (p + 1) * half_k]

    pl.semaphore_wait(barrier, ndp - 1 + nt - 1)

    def w_copy(direction, slot, p, src):
        target = right if direction == 0 else left
        return rcopy(
            src, wbuf.at[slot, p], wsend.at[direction, slot, p], wrecv.at[slot, p], target, t
        )

    def w_wait(slot, p):
        rcopy(
            wbuf.at[slot, p], wbuf.at[slot, p], ysend, wrecv.at[slot, p], nbr, t
        ).wait_recv()

    def w_send(slot, p, src):
        @pl.when(has_right)
        def _():
            w_copy(0, slot, p, src).start()

        @pl.when(has_left)
        def _():
            w_copy(1, slot, p, src).start()

    def h_copy(src, a, b, i, dpi, ti):
        return rcopy(src, hidb.at[a, b], hsend.at[i], hrecv.at[a, b], dpi, ti)

    def h_wait(a, b):
        h_copy(hidb.at[a, b], a, b, 0, nbr, t).wait_recv()

    y_copy = rcopy(wp_ref.at[oy], wbuf.at[zi, y], ysend, wrecv.at[zi, y], nbr, t)
    m_copy = rcopy(mask_ref, maskb.at[y], msem.at[0], msem.at[1], nbr, t)
    sends = [
        h_copy(hid_ref, y, t, 0, nbr, t),
        h_copy(hid_ref, y, t, 1, me, x_t),
        h_copy(hid_ref, y, t, 2, me, core_t),
        h_copy(hidb.at[oy, t], oy, t, 3, me, x_t),
        h_copy(hidb.at[oy, t], oy, t, 4, me, core_t),
        h_copy(hidb.at[y, x_t], y, x_t, 5, me, core_t),
        h_copy(hidb.at[oy, x_t], oy, x_t, 6, me, core_t),
    ]
    y_copy.start()
    w_send(zi, y, wp_ref.at[y])
    sends[1].start()
    sends[2].start()

    hidb[y, t] = hid_ref[...]
    maskb[y] = mask_ref[...]
    wbuf[zi, y] = wp_ref[y]
    for k in range(pieces):
        wob[me, k] = wo_ref[:, k * wide : (k + 1) * wide]
    acc[...] = jnp.zeros_like(acc)

    w_wait(zi, oy)
    w_send(zi, oy, wbuf.at[zi, oy])
    sends[0].start()
    m_copy.start()
    h_wait(y, x_t)
    sends[5].start()

    def o_copy(kind, z, k):
        target = (right, left, nbr)[kind]
        piece = wob.at[2 * z + y, k]
        return rcopy(
            piece, piece, osend.at[kind, z, k], orecv.at[2 * z + y, k], target, t
        )

    def o_wait(slot, k):
        piece = wob.at[slot, k]
        rcopy(piece, piece, osend.at[2, 0, k], orecv.at[slot, k], nbr, t).wait_recv()

    def forward(s):
        lo = zi - s
        hi = zi + s

        for p in range(2):

            @pl.when(lo >= 0)
            def _():
                w_wait(lo, p)

                @pl.when(has_right)
                def _():
                    w_copy(0, lo, p, wbuf.at[lo, p]).start()

            @pl.when(hi < nz)
            def _():
                w_wait(hi, p)

                @pl.when(has_left)
                def _():
                    w_copy(1, hi, p, wbuf.at[hi, p]).start()

    tile = 256

    def multiply(slot):
        for p in range(2):
            first = (slot * 2 + p) * rows
            block = first // cw
            off = pl.multiple_of(lax.rem(first, cw), 128)

            def step(i, carry):
                b = i // (length // tile)
                r = pl.multiple_of(lax.rem(i, length // tile) * tile, tile)
                acc[b, pl.ds(r, tile), :] += jnp.dot(
                    hidb[b, block, pl.ds(r, tile), pl.ds(off, rows)],
                    wbuf[slot, p],
                    preferred_element_type=jnp.float32,
                )
                return carry

            lax.fori_loop(0, 2 * (length // tile), step, 0)

    def multiply_pair(s):
        @pl.when(zi - s >= 0)
        def _():
            multiply(zi - s)

        @pl.when(zi + s < nz)
        def _():
            multiply(zi + s)

    forward(1)
    h_wait(oy, t)
    sends[3].start()
    sends[4].start()
    for k in range(pieces):
        o_copy(2, zi, k).start()

    ones = jnp.ones((8, cw), jnp.bfloat16)

    def row_sums(x):
        x = x.astype(jnp.float32)
        square = x * x
        high = square.astype(jnp.bfloat16)
        low = (square - high.astype(jnp.float32)).astype(jnp.bfloat16)
        return lax.dot_general(
            ones, high, NT_DIMS, preferred_element_type=jnp.float32
        ) + lax.dot_general(ones, low, NT_DIMS, preferred_element_type=jnp.float32)

    def over_tensor(d, src, dst, ss, rs):
        return rcopy(
            src, dst.at[d - 1], ss.at[d - 1], rs.at[d - 1], me, lax.rem(t + d, nt)
        )

    q_load.wait()
    count = qbuf.shape[0]

    def query_norm(i, carry):
        r = pl.multiple_of(i * 128, 128)
        qown[:, pl.ds(r, 128)] = row_sums(qbuf[pl.ds(r, 128), :])
        return carry

    lax.fori_loop(0, count // 128, query_norm, 0)
    q_copies = [over_tensor(d, qown, qrec, qsend, qrecv) for d in range(1, nt)]
    h_wait(oy, x_t)
    sends[6].start()
    for copy in q_copies:
        copy.start()
    for a, b in ((y, core_t), (oy, core_t)):
        h_wait(a, b)
    x_core = lax.rem(core_t + 2, nt)
    for a, b in ((y, x_core), (oy, x_core)):
        h_wait(a, b)
    for copy in sends:
        copy.wait_send()

    norm_rows = 64

    def normalise(i, carry):
        b = i // (length // norm_rows)
        r = pl.multiple_of(lax.rem(i, length // norm_rows) * norm_rows, norm_rows)
        total = jnp.zeros((norm_rows, 1), jnp.float32)
        for k in range(nt):
            x = hidb[b, k, pl.ds(r, norm_rows), :].astype(jnp.float32)
            total += jnp.sum(x * x, axis=-1, keepdims=True)
        factor = lax.rsqrt(total / d_model + EPS)
        for k in range(nt):
            x = hidb[b, k, pl.ds(r, norm_rows), :].astype(jnp.float32)
            g = gain_ref[k * cw : (k + 1) * cw].astype(jnp.float32)[None, :]
            hidb[b, k, pl.ds(r, norm_rows), :] = (x * factor * g).astype(jnp.bfloat16)
        return carry

    lax.fori_loop(0, 2 * (length // norm_rows), normalise, 0)

    multiply(zi)

    def later(s, carry):
        forward(s)
        multiply_pair(s - 1)
        return carry

    lax.fori_loop(2, nz, later, 0)

    for k in range(pieces):

        @pl.when(has_right)
        def _():
            o_copy(0, zi, k).start()

        @pl.when(has_left)
        def _():
            o_copy(1, zi, k).start()

    multiply_pair(nz - 1)
    m_copy.wait()

    def rotate(x):
        return (x * cos_ref[...] + pltpu.roll(x, HEAD // 2, 1) * sin_ref[...]).astype(
            jnp.bfloat16
        )

    def attend(b, out):
        key = rotate(acc[b, :, half_q : half_q + HEAD])
        val = acc[b, :, half_q + HEAD : half_q + 2 * HEAD].astype(jnp.bfloat16)
        keep = maskb[b] > 0
        for j in range(heads):
            qr = rotate(acc[b, :, j * HEAD : (j + 1) * HEAD])
            logits = lax.dot_general(qr, key, NT_DIMS, preferred_element_type=jnp.float32)
            logits = jnp.where(keep, logits * HEAD**-0.5, -1e30)
            e = jnp.exp(logits - jnp.max(logits, axis=-1, keepdims=True))
            w = (e * (1.0 / jnp.sum(e, axis=-1, keepdims=True))).astype(jnp.bfloat16)
            o = jnp.dot(w, val, preferred_element_type=jnp.float32).astype(jnp.bfloat16)
            out[:, j * HEAD : (j + 1) * HEAD] = o

    attend(oy, atts)
    a_copy = rcopy(atts, att.at[y], asem.at[0], asem.at[1], nbr, t)
    a_copy.start()
    attend(y, att.at[y])
    a_copy.wait()

    def r_copy(c, k):
        owner = c // nb
        d = lax.rem(owner - t + nt, nt)
        return rcopy(
            rss.at[c, k], rsr.at[d - 1, lax.rem(c, nb), k], rsend.at[c, k],
            rrecv.at[d - 1, lax.rem(c, nb), k], me, owner,
        )

    def project(c, k):
        mine = c // nb == t
        term = jnp.dot(
            att[0], wob[c, k, 0:half_q, :], preferred_element_type=jnp.float32
        ) + jnp.dot(
            att[1], wob[c, k, half_q : 2 * half_q, :], preferred_element_type=jnp.float32
        )

        @pl.when(mine)
        def _():
            hsum[lax.rem(c, nb), k] = term

        @pl.when(jnp.logical_not(mine))
        def _():
            rss[c, k] = term.astype(jnp.bfloat16)
            r_copy(c, k).start()

    def other(z, k):
        @pl.when((z >= 0) & (z < nz))
        def _():
            o_wait(2 * z + oy, k)
            project(2 * z + oy, k)

    def first(k, carry):
        project(me, k)
        other(zi, k)
        return carry

    lax.fori_loop(0, pieces, first, 0)

    def o_step(i, carry):
        s = 1 + i // pieces
        k = lax.rem(i, pieces)
        lo = zi - s
        hi = zi + s

        @pl.when(lo >= 0)
        def _():
            o_wait(2 * lo + y, k)

            @pl.when(has_right)
            def _():
                o_copy(0, lo, k).start()

            o_copy(2, lo, k).start()

        @pl.when(hi < nz)
        def _():
            o_wait(2 * hi + y, k)

            @pl.when(has_left)
            def _():
                o_copy(1, hi, k).start()

            o_copy(2, hi, k).start()

        @pl.when(lo >= 0)
        def _():
            project(2 * lo + y, k)

        @pl.when(hi < nz)
        def _():
            project(2 * hi + y, k)

        @pl.when(i > 0)
        def _():
            before = 1 + (i - 1) // pieces
            other(zi - before, lax.rem(i - 1, pieces))
            other(zi + before, lax.rem(i - 1, pieces))

        return carry

    lax.fori_loop(0, (nz - 1) * pieces, o_step, 0)
    other(zi - nz + 1, pieces - 1)
    other(zi + nz - 1, pieces - 1)

    for cb in range(nb):
        for k in range(pieces):
            for d in range(1, nt):
                rcopy(
                    rss.at[0, k], rsr.at[d - 1, cb, k], rsend.at[0, k],
                    rrecv.at[d - 1, cb, k], me, lax.rem(t + d, nt),
                ).wait_recv()

    def add_terms(i, carry):
        r = pl.multiple_of(i * 128, 128)
        part = pl.ds(r, 128)
        for j in range(nb * pieces):
            cols = slice(j * wide, (j + 1) * wide)
            total = hsum[j // pieces, j % pieces, part, :]
            for d in range(1, nt):
                total += rsr[d - 1, j // pieces, j % pieces, part, :].astype(jnp.float32)
            hbuf[part, cols] = (hid_ref[part, cols].astype(jnp.float32) + total).astype(
                jnp.bfloat16
            )
        fown[:, part] = row_sums(hbuf[part, :])
        return carry

    lax.fori_loop(0, length // 128, add_terms, 0)
    f_copies = [over_tensor(d, fown, frec, fsend, frecv) for d in range(1, nt)]
    for copy in f_copies:
        copy.start()
    mask_row = mask_ref[...].astype(jnp.float32)
    tokens = jnp.sum(mask_row, axis=1, keepdims=True)
    mask_rows = jnp.broadcast_to(mask_row, (8, length)).astype(jnp.bfloat16)
    for copy in f_copies:
        copy.wait_recv()
    squares = fown[0:1, :]
    for d in range(1, nt):
        squares += frec[d - 1][0:1, :]
    factor_row = lax.rsqrt(squares / d_model + EPS)
    colb[...] = jnp.broadcast_to(factor_row, (128, length)).T

    def final_norm(i, carry):
        r = pl.multiple_of(i * norm_rows, norm_rows)
        part = pl.ds(r, norm_rows)
        x = hbuf[part, :].astype(jnp.float32)
        g = fgain_ref[...].astype(jnp.float32)[None, :]
        hbuf[part, :] = (x * colb[part, 0:1] * g).astype(jnp.bfloat16)
        return carry

    lax.fori_loop(0, length // norm_rows, final_norm, 0)

    for j in range(cw // HEAD):
        cols = slice(j * HEAD, (j + 1) * HEAD)
        hn = hbuf[:, cols]
        lat = lat_ref[:, cols]
        logits = lax.dot_general(lat, hn, NT_DIMS, preferred_element_type=jnp.float32)
        logits = logits * HEAD**-0.5
        e = jnp.exp(logits - jnp.max(logits, axis=0, keepdims=True))
        w = (e * (1.0 / jnp.sum(e, axis=0, keepdims=True))).astype(jnp.bfloat16)
        seen = lax.dot_general(mask_rows, w, NT_DIMS, preferred_element_type=jnp.float32)
        high = seen.astype(jnp.bfloat16)
        low = (seen - high.astype(jnp.float32)).astype(jnp.bfloat16)
        total = (
            jnp.dot(mask_rows, hn, preferred_element_type=jnp.float32)
            + jnp.dot(high, lat, preferred_element_type=jnp.float32)
            + jnp.dot(low, lat, preferred_element_type=jnp.float32)
        )
        prow[me, :, cols] = total / tokens

    def p_copy(d):
        return rcopy(
            prow.at[me], prow.at[me], psend.at[d - 1], precv.at[me], lax.rem(me + d, ndp), t
        )

    def p_start(d, carry):
        p_copy(d).start()
        return carry

    def p_wait(d, carry):
        src = lax.rem(me + d, ndp)
        rcopy(
            prow.at[src], prow.at[src], psend.at[d - 1], precv.at[src], src, t
        ).wait_recv()
        return carry

    lax.fori_loop(1, ndp, p_start, 0)
    lax.fori_loop(1, ndp, p_wait, 0)
    every = jnp.concatenate([prow[i, 0:1, :] for i in range(ndp)], axis=0)
    sown[:, count:] = jnp.broadcast_to(
        jnp.sum(every * every, axis=1, keepdims=True), (ndp, 128)
    )
    every = every.astype(jnp.bfloat16)

    def score(i, carry):
        r = pl.multiple_of(i * 256, 256)
        sown[:, pl.ds(r, 256)] = lax.dot_general(
            every, qbuf[pl.ds(r, 256), :], NT_DIMS, preferred_element_type=jnp.float32
        )
        return carry

    lax.fori_loop(0, count // 256, score, 0)
    s_copies = [over_tensor(d, sown, srec, ssend, srecv) for d in range(1, nt)]
    for copy in s_copies:
        copy.start()
    for copy in q_copies + s_copies:
        copy.wait_recv()
    scores = sown[...]
    query_sq = qown[0:1, :]
    for d in range(1, nt):
        scores += srec[d - 1]
        query_sq += qrec[d - 1][0:1, :]
    similarity = (
        scores[:, :count]
        * lax.rsqrt(scores[:, count : count + 1] + 1e-06)
        * (lax.rsqrt(query_sq + 1e-06) / logit_divisor)
    )
    sim_ref[...] = similarity
    top = jnp.max(similarity, axis=0, keepdims=True)
    norm_ref[...] = top + jnp.log(jnp.sum(jnp.exp(similarity - top), axis=0, keepdims=True))

    for copy in f_copies + q_copies + s_copies:
        copy.wait_send()

    def p_drain(d, carry):
        p_copy(d).wait_send()
        return carry

    lax.fori_loop(1, ndp, p_drain, 0)

    y_copy.wait_send()

    def drain(z, carry):
        for k in range(pieces):
            o_copy(2, z, k).wait_send()

        @pl.when(has_right & (z <= zi))
        def _():
            for k in range(pieces):
                o_copy(0, z, k).wait_send()
            for p in range(2):
                w_copy(0, z, p, wbuf.at[z, p]).wait_send()

        @pl.when(has_left & (z >= zi))
        def _():
            for k in range(pieces):
                o_copy(1, z, k).wait_send()
            for p in range(2):
                w_copy(1, z, p, wbuf.at[z, p]).wait_send()

        return carry

    lax.fori_loop(0, nz, drain, 0)

    def drain_terms(c, carry):
        @pl.when(c // nb != t)
        def _():
            for k in range(pieces):
                r_copy(c, k).wait_send()

        return carry

    lax.fori_loop(0, ndp, drain_terms, 0)


def layer(ndp, nt, rows, mask, wq, wk, wv, wo, gain, cosine, sine, fgain, lat, queries):
    length, cw = rows.shape
    depth = wq.shape[0]
    pack = (wq.shape[1] + wk.shape[1] + wv.shape[1]) // 2
    half_q = wo.shape[0] // 2
    nz, nb = ndp // 2, ndp // nt
    wide = 128
    pieces = wo.shape[1] // wide
    count = queries.shape[0]
    dma = pltpu.SemaphoreType.DMA
    bf, f32 = jnp.bfloat16, jnp.float32
    vmem = pl.BlockSpec(memory_space=pltpu.VMEM)
    return pl.pallas_call(
        functools.partial(layer_kernel, ndp, nt),
        out_shape=(
            jax.ShapeDtypeStruct((ndp, count), f32),
            jax.ShapeDtypeStruct((1, count), f32),
        ),
        in_specs=[vmem] * 11 + [pl.BlockSpec(memory_space=pl.ANY)],
        out_specs=(vmem, vmem),
        scratch_shapes=[
            pltpu.VMEM((2, nt, length, cw), bf),
            pltpu.VMEM((2,) + mask.shape, mask.dtype),
            pltpu.VMEM((2, depth, pack), bf),
            pltpu.VMEM((nz, 2, depth, pack), bf),
            pltpu.VMEM((ndp, pieces, wo.shape[0], wide), bf),
            pltpu.VMEM((2, length, pack), f32),
            pltpu.VMEM((length, half_q), bf),
            pltpu.VMEM((2, length, half_q), bf),
            pltpu.VMEM((ndp, pieces, length, wide), bf),
            pltpu.VMEM((nt - 1, nb, pieces, length, wide), bf),
            pltpu.VMEM((nb, pieces, length, wide), f32),
            pltpu.VMEM((length, cw), bf),
            pltpu.VMEM((length, 128), f32),
            pltpu.VMEM((8, length), f32),
            pltpu.VMEM((nt - 1, 8, length), f32),
            pltpu.VMEM((count, cw), bf),
            pltpu.VMEM((8, count), f32),
            pltpu.VMEM((nt - 1, 8, count), f32),
            pltpu.VMEM((ndp, 8, cw), f32),
            pltpu.VMEM((ndp, count + 128), f32),
            pltpu.VMEM((nt - 1, ndp, count + 128), f32),
            dma((7,)),
            dma((2, nt)),
            dma((2,)),
            dma,
            dma((2, nz, 2)),
            dma((nz, 2)),
            dma((2,)),
            dma((3, nz, pieces)),
            dma((ndp, pieces)),
            dma((ndp, pieces)),
            dma((nt - 1, nb, pieces)),
            dma((nt - 1,)),
            dma((nt - 1,)),
            dma,
            dma((nt - 1,)),
            dma((nt - 1,)),
            dma((ndp - 1,)),
            dma((ndp,)),
            dma((nt - 1,)),
            dma((nt - 1,)),
        ],
        compiler_params=pltpu.CompilerParams(
            collective_id=0, has_side_effects=True, vmem_limit_bytes=60 * 1024 * 1024
        ),
    )(rows, mask, wq, wk, wv, wo, gain, cosine, sine, fgain, lat, queries)


def local(
    ndp, nt,
    hidden_in, norm_gain, w_query, w_key, w_value, w_out, final_gain, latents, token_mask, queries,
):
    _, length, part_width = hidden_in.shape
    rows = hidden_in.reshape(length, part_width)
    half = HEAD // 2
    freqs = np.float32(10000.0) ** (-2.0 * np.arange(half, dtype=np.float32) / HEAD)
    angle = np.arange(length, dtype=np.float32)[:, None] * freqs.astype(np.float32)[None, :]
    cosine = jnp.asarray(np.concatenate([np.cos(angle)] * 2, axis=1), jnp.float32)
    sine = jnp.asarray(np.concatenate([-np.sin(angle), np.sin(angle)], axis=1), jnp.float32)
    similarity, log_norm = layer(
        ndp, nt, rows, token_mask, w_query, w_key, w_value, w_out, norm_gain, cosine, sine, final_gain,
        latents, queries,
    )
    return similarity.T, log_norm[0]


def solution(mesh):
    placed = (
        P("dp", None, "tensor"),
        P(),
        P("dp", "tensor"),
        P("dp", "tensor"),
        P("dp", "tensor"),
        P("tensor", "dp"),
        P("tensor"),
        P(None, "tensor"),
        P("dp", None),
        P("dp", "tensor"),
    )
    return jax.shard_map(
        functools.partial(local, mesh.shape["dp"], mesh.shape["tensor"]),
        mesh=mesh, in_specs=placed, out_specs=(P("dp", None), P("dp")), check_vma=False,
    )
```

```python
import functools

import jax
import jax.numpy as jnp
import numpy as np
from jax import lax
from jax.experimental import pallas as pl
from jax.experimental.pallas import tpu as pltpu
from jax.sharding import PartitionSpec as P

HEAD = 128
EPS = 1e-05
logit_divisor = 0.02
MESH = pl.DeviceIdType.MESH
NT_DIMS = (((1,), (1,)), ((), ()))


def layer_kernel(
    ndp, nt,
    hid_ref, mask_ref, wq_ref, wk_ref, wv_ref, wo_ref, gain_ref, cos_ref, sin_ref,
    fgain_ref, lat_ref, query_ref,
    sim_ref, norm_ref,
    hidb, maskb, wp_ref, wbuf, wob, acc, atts, att, rss, rsr, hsum,
    hbuf, colb, fown, frec, qbuf, qown, qrec, prow, sown, srec,
    hsend, hrecv, msem, ysend, wsend, wrecv, asem, osend, orecv, rsend, rrecv,
    fsend, frecv, qload, qsend, qrecv, psend, precv, ssend, srecv,
):
    nz = ndp // 2
    nb = ndp // nt
    pieces, _, wide = wob.shape[1:]
    length, cw = hid_ref.shape
    rows = wq_ref.shape[0]
    half_q = att.shape[2]
    heads = half_q // HEAD
    d_model = cw * nt
    me = lax.axis_index("dp")
    t = lax.axis_index("tensor")
    zi = me // 2
    y = lax.rem(me, 2)
    oy = 1 - y
    nbr = 2 * zi + oy
    left = me - 2
    right = me + 2
    core_t = t + 1 - 2 * lax.rem(t, 2)
    x_t = lax.rem(t + 2, nt)
    has_left = zi > 0
    has_right = zi < nz - 1

    def rcopy(src, dst, ss, rs, dpi, ti):
        return pltpu.make_async_remote_copy(
            src_ref=src, dst_ref=dst, send_sem=ss, recv_sem=rs,
            device_id=(dpi, ti), device_id_type=MESH,
        )

    q_load = pltpu.make_async_copy(query_ref, qbuf, qload)
    q_load.start()

    barrier = pltpu.get_barrier_semaphore()

    def greet(d, carry):
        pl.semaphore_signal(
            barrier, inc=1, device_id=(lax.rem(me + d, ndp), t), device_id_type=MESH
        )
        return carry

    lax.fori_loop(1, ndp, greet, 0)
    for d in range(1, nt):
        pl.semaphore_signal(
            barrier, inc=1, device_id=(me, lax.rem(t + d, nt)), device_id_type=MESH
        )

    half_k = wk_ref.shape[1] // 2
    for p in range(2):
        wp_ref[p, :, 0:half_q] = wq_ref[:, p * half_q : (p + 1) * half_q]
        wp_ref[p, :, half_q : half_q + half_k] = wk_ref[:, p * half_k : (p + 1) * half_k]
        wp_ref[p, :, half_q + half_k :] = wv_ref[:, p * half_k : (p + 1) * half_k]

    pl.semaphore_wait(barrier, ndp - 1 + nt - 1)

    def w_copy(direction, slot, p, src):
        target = right if direction == 0 else left
        return rcopy(
            src, wbuf.at[slot, p], wsend.at[direction, slot, p], wrecv.at[slot, p], target, t
        )

    def w_wait(slot, p):
        rcopy(
            wbuf.at[slot, p], wbuf.at[slot, p], ysend, wrecv.at[slot, p], nbr, t
        ).wait_recv()

    def w_send(slot, p, src):
        @pl.when(has_right)
        def _():
            w_copy(0, slot, p, src).start()

        @pl.when(has_left)
        def _():
            w_copy(1, slot, p, src).start()

    def h_copy(src, a, b, i, dpi, ti):
        return rcopy(src, hidb.at[a, b], hsend.at[i], hrecv.at[a, b], dpi, ti)

    def h_wait(a, b):
        h_copy(hidb.at[a, b], a, b, 0, nbr, t).wait_recv()

    y_copy = rcopy(wp_ref.at[oy], wbuf.at[zi, y], ysend, wrecv.at[zi, y], nbr, t)
    m_copy = rcopy(mask_ref, maskb.at[y], msem.at[0], msem.at[1], nbr, t)
    sends = [
        h_copy(hid_ref, y, t, 0, nbr, t),
        h_copy(hid_ref, y, t, 1, me, x_t),
        h_copy(hid_ref, y, t, 2, me, core_t),
        h_copy(hidb.at[oy, t], oy, t, 3, me, x_t),
        h_copy(hidb.at[oy, t], oy, t, 4, me, core_t),
        h_copy(hidb.at[y, x_t], y, x_t, 5, me, core_t),
        h_copy(hidb.at[oy, x_t], oy, x_t, 6, me, core_t),
    ]
    y_copy.start()
    w_send(zi, y, wp_ref.at[y])
    sends[1].start()
    sends[2].start()

    hidb[y, t] = hid_ref[...]
    maskb[y] = mask_ref[...]
    wbuf[zi, y] = wp_ref[y]
    for k in range(pieces):
        wob[me, k] = wo_ref[:, k * wide : (k + 1) * wide]
    acc[...] = jnp.zeros_like(acc)

    w_wait(zi, oy)
    w_send(zi, oy, wbuf.at[zi, oy])
    sends[0].start()
    m_copy.start()
    h_wait(y, x_t)
    sends[5].start()

    def o_copy(kind, z, k):
        target = (right, left, nbr)[kind]
        piece = wob.at[2 * z + y, k]
        return rcopy(
            piece, piece, osend.at[kind, z, k], orecv.at[2 * z + y, k], target, t
        )

    def o_wait(slot, k):
        piece = wob.at[slot, k]
        rcopy(piece, piece, osend.at[2, 0, k], orecv.at[slot, k], nbr, t).wait_recv()

    def forward(s):
        lo = zi - s
        hi = zi + s

        for p in range(2):

            @pl.when(lo >= 0)
            def _():
                w_wait(lo, p)

                @pl.when(has_right)
                def _():
                    w_copy(0, lo, p, wbuf.at[lo, p]).start()

            @pl.when(hi < nz)
            def _():
                w_wait(hi, p)

                @pl.when(has_left)
                def _():
                    w_copy(1, hi, p, wbuf.at[hi, p]).start()

    tile = 256

    def multiply(slot):
        for p in range(2):
            first = (slot * 2 + p) * rows
            block = first // cw
            off = pl.multiple_of(lax.rem(first, cw), 128)

            def step(i, carry):
                b = i // (length // tile)
                r = pl.multiple_of(lax.rem(i, length // tile) * tile, tile)
                acc[b, pl.ds(r, tile), :] += jnp.dot(
                    hidb[b, block, pl.ds(r, tile), pl.ds(off, rows)],
                    wbuf[slot, p],
                    preferred_element_type=jnp.float32,
                )
                return carry

            lax.fori_loop(0, 2 * (length // tile), step, 0)

    def multiply_pair(s):
        @pl.when(zi - s >= 0)
        def _():
            multiply(zi - s)

        @pl.when(zi + s < nz)
        def _():
            multiply(zi + s)

    forward(1)

    for k in range(pieces):

        @pl.when(has_right)
        def _():
            o_copy(0, zi, k).start()

        @pl.when(has_left)
        def _():
            o_copy(1, zi, k).start()

    h_wait(oy, t)
    sends[3].start()
    sends[4].start()
    for k in range(pieces):
        o_copy(2, zi, k).start()

    ones = jnp.ones((8, cw), jnp.bfloat16)

    def row_sums(x):
        x = x.astype(jnp.float32)
        square = x * x
        high = square.astype(jnp.bfloat16)
        low = (square - high.astype(jnp.float32)).astype(jnp.bfloat16)
        return lax.dot_general(
            ones, high, NT_DIMS, preferred_element_type=jnp.float32
        ) + lax.dot_general(ones, low, NT_DIMS, preferred_element_type=jnp.float32)

    def over_tensor(d, src, dst, ss, rs):
        return rcopy(
            src, dst.at[d - 1], ss.at[d - 1], rs.at[d - 1], me, lax.rem(t + d, nt)
        )

    q_load.wait()
    count = qbuf.shape[0]

    def query_norm(i, carry):
        r = pl.multiple_of(i * 128, 128)
        qown[:, pl.ds(r, 128)] = row_sums(qbuf[pl.ds(r, 128), :])
        return carry

    lax.fori_loop(0, count // 128, query_norm, 0)
    q_copies = [over_tensor(d, qown, qrec, qsend, qrecv) for d in range(1, nt)]
    h_wait(oy, x_t)
    sends[6].start()
    for copy in q_copies:
        copy.start()
    if nz > 2:
        forward(2)
    for a, b in ((y, core_t), (oy, core_t)):
        h_wait(a, b)
    x_core = lax.rem(core_t + 2, nt)
    for a, b in ((y, x_core), (oy, x_core)):
        h_wait(a, b)
    for copy in sends:
        copy.wait_send()

    norm_rows = 64

    def normalise(i, carry):
        b = i // (length // norm_rows)
        r = pl.multiple_of(lax.rem(i, length // norm_rows) * norm_rows, norm_rows)
        total = jnp.zeros((norm_rows, 1), jnp.float32)
        for k in range(nt):
            x = hidb[b, k, pl.ds(r, norm_rows), :].astype(jnp.float32)
            total += jnp.sum(x * x, axis=-1, keepdims=True)
        factor = lax.rsqrt(total / d_model + EPS)
        for k in range(nt):
            x = hidb[b, k, pl.ds(r, norm_rows), :].astype(jnp.float32)
            g = gain_ref[k * cw : (k + 1) * cw].astype(jnp.float32)[None, :]
            hidb[b, k, pl.ds(r, norm_rows), :] = (x * factor * g).astype(jnp.bfloat16)
        return carry

    lax.fori_loop(0, 2 * (length // norm_rows), normalise, 0)

    multiply(zi)

    if nz > 2:
        multiply_pair(1)

    def o_forward(s, k):
        lo = zi - s
        hi = zi + s

        @pl.when(lo >= 0)
        def _():
            o_wait(2 * lo + y, k)

            @pl.when(has_right)
            def _():
                o_copy(0, lo, k).start()

            o_copy(2, lo, k).start()

        @pl.when(hi < nz)
        def _():
            o_wait(2 * hi + y, k)

            @pl.when(has_left)
            def _():
                o_copy(1, hi, k).start()

            o_copy(2, hi, k).start()

    early = max(nz - 3, 0)

    def later(s, carry):
        def relay(k, inner):
            o_forward(s - 2, k)
            return inner

        lax.fori_loop(0, pieces, relay, 0)
        forward(s)
        multiply_pair(s - 1)
        return carry

    lax.fori_loop(3, nz, later, 0)
    multiply_pair(nz - 1)
    m_copy.wait()

    def rotate(x):
        return (x * cos_ref[...] + pltpu.roll(x, HEAD // 2, 1) * sin_ref[...]).astype(
            jnp.bfloat16
        )

    def attend(b, out):
        key = rotate(acc[b, :, half_q : half_q + HEAD])
        val = acc[b, :, half_q + HEAD : half_q + 2 * HEAD].astype(jnp.bfloat16)
        keep = maskb[b] > 0
        for j in range(heads):
            qr = rotate(acc[b, :, j * HEAD : (j + 1) * HEAD])
            logits = lax.dot_general(qr, key, NT_DIMS, preferred_element_type=jnp.float32)
            logits = jnp.where(keep, logits * HEAD**-0.5, -1e30)
            e = jnp.exp(logits - jnp.max(logits, axis=-1, keepdims=True))
            w = (e * (1.0 / jnp.sum(e, axis=-1, keepdims=True))).astype(jnp.bfloat16)
            o = jnp.dot(w, val, preferred_element_type=jnp.float32).astype(jnp.bfloat16)
            out[:, j * HEAD : (j + 1) * HEAD] = o

    attend(oy, atts)
    a_copy = rcopy(atts, att.at[y], asem.at[0], asem.at[1], nbr, t)
    a_copy.start()
    attend(y, att.at[y])
    a_copy.wait()

    def r_copy(c, k):
        owner = c // nb
        d = lax.rem(owner - t + nt, nt)
        return rcopy(
            rss.at[c, k], rsr.at[d - 1, lax.rem(c, nb), k], rsend.at[c, k],
            rrecv.at[d - 1, lax.rem(c, nb), k], me, owner,
        )

    def project(c, k):
        mine = c // nb == t
        term = jnp.dot(
            att[0], wob[c, k, 0:half_q, :], preferred_element_type=jnp.float32
        ) + jnp.dot(
            att[1], wob[c, k, half_q : 2 * half_q, :], preferred_element_type=jnp.float32
        )

        @pl.when(mine)
        def _():
            hsum[lax.rem(c, nb), k] = term

        @pl.when(jnp.logical_not(mine))
        def _():
            rss[c, k] = term.astype(jnp.bfloat16)
            r_copy(c, k).start()

    def other(z, k):
        @pl.when((z >= 0) & (z < nz))
        def _():
            o_wait(2 * z + oy, k)
            project(2 * z + oy, k)

    def first(k, carry):
        project(me, k)
        other(zi, k)
        return carry

    lax.fori_loop(0, pieces, first, 0)

    def project_pair(s, k):
        @pl.when(zi - s >= 0)
        def _():
            project(2 * (zi - s) + y, k)

        @pl.when(zi + s < nz)
        def _():
            project(2 * (zi + s) + y, k)

    def arrived(i, carry):
        s = 1 + i // pieces
        k = lax.rem(i, pieces)
        project_pair(s, k)
        other(zi - s, k)
        other(zi + s, k)
        return carry

    lax.fori_loop(0, early * pieces, arrived, 0)

    def o_step(i, carry):
        s = 1 + i // pieces
        k = lax.rem(i, pieces)
        o_forward(s, k)
        project_pair(s, k)

        @pl.when(i > early * pieces)
        def _():
            before = 1 + (i - 1) // pieces
            other(zi - before, lax.rem(i - 1, pieces))
            other(zi + before, lax.rem(i - 1, pieces))

        return carry

    lax.fori_loop(early * pieces, (nz - 1) * pieces, o_step, 0)
    other(zi - nz + 1, pieces - 1)
    other(zi + nz - 1, pieces - 1)

    for cb in range(nb):
        for k in range(pieces):
            for d in range(1, nt):
                rcopy(
                    rss.at[0, k], rsr.at[d - 1, cb, k], rsend.at[0, k],
                    rrecv.at[d - 1, cb, k], me, lax.rem(t + d, nt),
                ).wait_recv()

    def add_terms(i, carry):
        r = pl.multiple_of(i * 128, 128)
        part = pl.ds(r, 128)
        for j in range(nb * pieces):
            cols = slice(j * wide, (j + 1) * wide)
            total = hsum[j // pieces, j % pieces, part, :]
            for d in range(1, nt):
                total += rsr[d - 1, j // pieces, j % pieces, part, :].astype(jnp.float32)
            hbuf[part, cols] = (hid_ref[part, cols].astype(jnp.float32) + total).astype(
                jnp.bfloat16
            )
        fown[:, part] = row_sums(hbuf[part, :])
        return carry

    lax.fori_loop(0, length // 128, add_terms, 0)
    f_copies = [over_tensor(d, fown, frec, fsend, frecv) for d in range(1, nt)]
    for copy in f_copies:
        copy.start()
    mask_row = mask_ref[...].astype(jnp.float32)
    tokens = jnp.sum(mask_row, axis=1, keepdims=True)
    mask_rows = jnp.broadcast_to(mask_row, (8, length)).astype(jnp.bfloat16)
    for copy in f_copies:
        copy.wait_recv()
    squares = fown[0:1, :]
    for d in range(1, nt):
        squares += frec[d - 1][0:1, :]
    factor_row = lax.rsqrt(squares / d_model + EPS)
    colb[...] = jnp.broadcast_to(factor_row, (128, length)).T

    def final_norm(i, carry):
        r = pl.multiple_of(i * norm_rows, norm_rows)
        part = pl.ds(r, norm_rows)
        x = hbuf[part, :].astype(jnp.float32)
        g = fgain_ref[...].astype(jnp.float32)[None, :]
        hbuf[part, :] = (x * colb[part, 0:1] * g).astype(jnp.bfloat16)
        return carry

    lax.fori_loop(0, length // norm_rows, final_norm, 0)

    for j in range(cw // HEAD):
        cols = slice(j * HEAD, (j + 1) * HEAD)
        hn = hbuf[:, cols]
        lat = lat_ref[:, cols]
        logits = lax.dot_general(lat, hn, NT_DIMS, preferred_element_type=jnp.float32)
        logits = logits * HEAD**-0.5
        e = jnp.exp(logits - jnp.max(logits, axis=0, keepdims=True))
        w = (e * (1.0 / jnp.sum(e, axis=0, keepdims=True))).astype(jnp.bfloat16)
        seen = lax.dot_general(mask_rows, w, NT_DIMS, preferred_element_type=jnp.float32)
        high = seen.astype(jnp.bfloat16)
        low = (seen - high.astype(jnp.float32)).astype(jnp.bfloat16)
        total = (
            jnp.dot(mask_rows, hn, preferred_element_type=jnp.float32)
            + jnp.dot(high, lat, preferred_element_type=jnp.float32)
            + jnp.dot(low, lat, preferred_element_type=jnp.float32)
        )
        prow[me, :, cols] = total / tokens

    def p_copy(d):
        return rcopy(
            prow.at[me], prow.at[me], psend.at[d - 1], precv.at[me], lax.rem(me + d, ndp), t
        )

    def p_start(d, carry):
        p_copy(d).start()
        return carry

    def p_wait(d, carry):
        src = lax.rem(me + d, ndp)
        rcopy(
            prow.at[src], prow.at[src], psend.at[d - 1], precv.at[src], src, t
        ).wait_recv()
        return carry

    lax.fori_loop(1, ndp, p_start, 0)
    lax.fori_loop(1, ndp, p_wait, 0)
    every = jnp.concatenate([prow[i, 0:1, :] for i in range(ndp)], axis=0)
    sown[:, count:] = jnp.broadcast_to(
        jnp.sum(every * every, axis=1, keepdims=True), (ndp, 128)
    )
    every = every.astype(jnp.bfloat16)

    def score(i, carry):
        r = pl.multiple_of(i * 256, 256)
        sown[:, pl.ds(r, 256)] = lax.dot_general(
            every, qbuf[pl.ds(r, 256), :], NT_DIMS, preferred_element_type=jnp.float32
        )
        return carry

    lax.fori_loop(0, count // 256, score, 0)
    s_copies = [over_tensor(d, sown, srec, ssend, srecv) for d in range(1, nt)]
    for copy in s_copies:
        copy.start()
    for copy in q_copies + s_copies:
        copy.wait_recv()
    scores = sown[...]
    query_sq = qown[0:1, :]
    for d in range(1, nt):
        scores += srec[d - 1]
        query_sq += qrec[d - 1][0:1, :]
    similarity = (
        scores[:, :count]
        * lax.rsqrt(scores[:, count : count + 1] + 1e-06)
        * (lax.rsqrt(query_sq + 1e-06) / logit_divisor)
    )
    sim_ref[...] = similarity
    top = jnp.max(similarity, axis=0, keepdims=True)
    norm_ref[...] = top + jnp.log(jnp.sum(jnp.exp(similarity - top), axis=0, keepdims=True))

    for copy in f_copies + q_copies + s_copies:
        copy.wait_send()

    def p_drain(d, carry):
        p_copy(d).wait_send()
        return carry

    lax.fori_loop(1, ndp, p_drain, 0)

    y_copy.wait_send()

    def drain(z, carry):
        for k in range(pieces):
            o_copy(2, z, k).wait_send()

        @pl.when(has_right & (z <= zi))
        def _():
            for k in range(pieces):
                o_copy(0, z, k).wait_send()
            for p in range(2):
                w_copy(0, z, p, wbuf.at[z, p]).wait_send()

        @pl.when(has_left & (z >= zi))
        def _():
            for k in range(pieces):
                o_copy(1, z, k).wait_send()
            for p in range(2):
                w_copy(1, z, p, wbuf.at[z, p]).wait_send()

        return carry

    lax.fori_loop(0, nz, drain, 0)

    def drain_terms(c, carry):
        @pl.when(c // nb != t)
        def _():
            for k in range(pieces):
                r_copy(c, k).wait_send()

        return carry

    lax.fori_loop(0, ndp, drain_terms, 0)


def layer(ndp, nt, rows, mask, wq, wk, wv, wo, gain, cosine, sine, fgain, lat, queries):
    length, cw = rows.shape
    depth = wq.shape[0]
    pack = (wq.shape[1] + wk.shape[1] + wv.shape[1]) // 2
    half_q = wo.shape[0] // 2
    nz, nb = ndp // 2, ndp // nt
    wide = 128
    pieces = wo.shape[1] // wide
    count = queries.shape[0]
    dma = pltpu.SemaphoreType.DMA
    bf, f32 = jnp.bfloat16, jnp.float32
    vmem = pl.BlockSpec(memory_space=pltpu.VMEM)
    return pl.pallas_call(
        functools.partial(layer_kernel, ndp, nt),
        out_shape=(
            jax.ShapeDtypeStruct((ndp, count), f32),
            jax.ShapeDtypeStruct((1, count), f32),
        ),
        in_specs=[vmem] * 11 + [pl.BlockSpec(memory_space=pl.ANY)],
        out_specs=(vmem, vmem),
        scratch_shapes=[
            pltpu.VMEM((2, nt, length, cw), bf),
            pltpu.VMEM((2,) + mask.shape, mask.dtype),
            pltpu.VMEM((2, depth, pack), bf),
            pltpu.VMEM((nz, 2, depth, pack), bf),
            pltpu.VMEM((ndp, pieces, wo.shape[0], wide), bf),
            pltpu.VMEM((2, length, pack), f32),
            pltpu.VMEM((length, half_q), bf),
            pltpu.VMEM((2, length, half_q), bf),
            pltpu.VMEM((ndp, pieces, length, wide), bf),
            pltpu.VMEM((nt - 1, nb, pieces, length, wide), bf),
            pltpu.VMEM((nb, pieces, length, wide), f32),
            pltpu.VMEM((length, cw), bf),
            pltpu.VMEM((length, 128), f32),
            pltpu.VMEM((8, length), f32),
            pltpu.VMEM((nt - 1, 8, length), f32),
            pltpu.VMEM((count, cw), bf),
            pltpu.VMEM((8, count), f32),
            pltpu.VMEM((nt - 1, 8, count), f32),
            pltpu.VMEM((ndp, 8, cw), f32),
            pltpu.VMEM((ndp, count + 128), f32),
            pltpu.VMEM((nt - 1, ndp, count + 128), f32),
            dma((7,)),
            dma((2, nt)),
            dma((2,)),
            dma,
            dma((2, nz, 2)),
            dma((nz, 2)),
            dma((2,)),
            dma((3, nz, pieces)),
            dma((ndp, pieces)),
            dma((ndp, pieces)),
            dma((nt - 1, nb, pieces)),
            dma((nt - 1,)),
            dma((nt - 1,)),
            dma,
            dma((nt - 1,)),
            dma((nt - 1,)),
            dma((ndp - 1,)),
            dma((ndp,)),
            dma((nt - 1,)),
            dma((nt - 1,)),
        ],
        compiler_params=pltpu.CompilerParams(
            collective_id=0, has_side_effects=True, vmem_limit_bytes=60 * 1024 * 1024
        ),
    )(rows, mask, wq, wk, wv, wo, gain, cosine, sine, fgain, lat, queries)


def local(
    ndp, nt,
    hidden_in, norm_gain, w_query, w_key, w_value, w_out, final_gain, latents, token_mask, queries,
):
    _, length, part_width = hidden_in.shape
    rows = hidden_in.reshape(length, part_width)
    half = HEAD // 2
    freqs = np.float32(10000.0) ** (-2.0 * np.arange(half, dtype=np.float32) / HEAD)
    angle = np.arange(length, dtype=np.float32)[:, None] * freqs.astype(np.float32)[None, :]
    cosine = jnp.asarray(np.concatenate([np.cos(angle)] * 2, axis=1), jnp.float32)
    sine = jnp.asarray(np.concatenate([-np.sin(angle), np.sin(angle)], axis=1), jnp.float32)
    similarity, log_norm = layer(
        ndp, nt, rows, token_mask, w_query, w_key, w_value, w_out, norm_gain, cosine, sine, final_gain,
        latents, queries,
    )
    return similarity.T, log_norm[0]


def solution(mesh):
    placed = (
        P("dp", None, "tensor"),
        P(),
        P("dp", "tensor"),
        P("dp", "tensor"),
        P("dp", "tensor"),
        P("tensor", "dp"),
        P("tensor"),
        P(None, "tensor"),
        P("dp", None),
        P("dp", "tensor"),
    )
    return jax.shard_map(
        functools.partial(local, mesh.shape["dp"], mesh.shape["tensor"]),
        mesh=mesh, in_specs=placed, out_specs=(P("dp", None), P("dp")), check_vma=False,
    )
```

```python
import functools

import jax
import jax.numpy as jnp
import numpy as np
from jax import lax
from jax.experimental import pallas as pl
from jax.experimental.pallas import tpu as pltpu
from jax.sharding import PartitionSpec as P

HEAD = 128
EPS = 1e-05
logit_divisor = 0.02
MESH = pl.DeviceIdType.MESH
NT_DIMS = (((1,), (1,)), ((), ()))


def layer_kernel(
    ndp, nt,
    hid_ref, mask_ref, wq_ref, wk_ref, wv_ref, wo_ref, gain_ref, cos_ref, sin_ref,
    fgain_ref, lat_ref, query_ref,
    sim_ref, norm_ref,
    hidb, maskb, wp_ref, wbuf, wob, acc, atts, att, rss, rsr, hsum,
    hbuf, colb, fown, frec, qbuf, qown, qrec, prow, sown, srec,
    hsend, hrecv, msem, ysend, wsend, wrecv, asem, osend, orecv, rsend, rrecv,
    fsend, frecv, qload, qsend, qrecv, psend, precv, ssend, srecv,
):
    nz = ndp // 2
    nb = ndp // nt
    pieces, _, wide = wob.shape[1:]
    length, cw = hid_ref.shape
    rows = wq_ref.shape[0]
    half_q = att.shape[2]
    heads = half_q // HEAD
    d_model = cw * nt
    me = lax.axis_index("dp")
    t = lax.axis_index("tensor")
    zi = me // 2
    y = lax.rem(me, 2)
    oy = 1 - y
    nbr = 2 * zi + oy
    left = me - 2
    right = me + 2
    core_t = t + 1 - 2 * lax.rem(t, 2)
    x_t = lax.rem(t + 2, nt)
    has_left = zi > 0
    has_right = zi < nz - 1

    def rcopy(src, dst, ss, rs, dpi, ti):
        return pltpu.make_async_remote_copy(
            src_ref=src, dst_ref=dst, send_sem=ss, recv_sem=rs,
            device_id=(dpi, ti), device_id_type=MESH,
        )

    q_load = pltpu.make_async_copy(query_ref, qbuf, qload)
    q_load.start()

    barrier = pltpu.get_barrier_semaphore()

    def greet(d, carry):
        pl.semaphore_signal(
            barrier, inc=1, device_id=(lax.rem(me + d, ndp), t), device_id_type=MESH
        )
        return carry

    lax.fori_loop(1, ndp, greet, 0)
    for d in range(1, nt):
        pl.semaphore_signal(
            barrier, inc=1, device_id=(me, lax.rem(t + d, nt)), device_id_type=MESH
        )

    half_k = wk_ref.shape[1] // 2
    for p in range(2):
        wp_ref[p, :, 0:half_q] = wq_ref[:, p * half_q : (p + 1) * half_q]
        wp_ref[p, :, half_q : half_q + half_k] = wk_ref[:, p * half_k : (p + 1) * half_k]
        wp_ref[p, :, half_q + half_k :] = wv_ref[:, p * half_k : (p + 1) * half_k]

    pl.semaphore_wait(barrier, ndp - 1 + nt - 1)

    def w_copy(direction, slot, p, src):
        target = right if direction == 0 else left
        return rcopy(
            src, wbuf.at[slot, p], wsend.at[direction, slot, p], wrecv.at[slot, p], target, t
        )

    def w_wait(slot, p):
        rcopy(
            wbuf.at[slot, p], wbuf.at[slot, p], ysend, wrecv.at[slot, p], nbr, t
        ).wait_recv()

    def w_send(slot, p, src):
        @pl.when(has_right)
        def _():
            w_copy(0, slot, p, src).start()

        @pl.when(has_left)
        def _():
            w_copy(1, slot, p, src).start()

    def h_copy(src, a, b, i, dpi, ti):
        return rcopy(src, hidb.at[a, b], hsend.at[i], hrecv.at[a, b], dpi, ti)

    def h_wait(a, b):
        h_copy(hidb.at[a, b], a, b, 0, nbr, t).wait_recv()

    y_copy = rcopy(wp_ref.at[oy], wbuf.at[zi, y], ysend, wrecv.at[zi, y], nbr, t)
    m_copy = rcopy(mask_ref, maskb.at[y], msem.at[0], msem.at[1], nbr, t)
    sends = [
        h_copy(hid_ref, y, t, 0, nbr, t),
        h_copy(hid_ref, y, t, 1, me, x_t),
        h_copy(hid_ref, y, t, 2, me, core_t),
        h_copy(hidb.at[oy, t], oy, t, 3, me, x_t),
        h_copy(hidb.at[oy, t], oy, t, 4, me, core_t),
        h_copy(hidb.at[y, x_t], y, x_t, 5, me, core_t),
        h_copy(hidb.at[oy, x_t], oy, x_t, 6, me, core_t),
    ]
    y_copy.start()
    w_send(zi, y, wp_ref.at[y])
    sends[1].start()
    sends[2].start()

    hidb[y, t] = hid_ref[...]
    maskb[y] = mask_ref[...]
    wbuf[zi, y] = wp_ref[y]
    for k in range(pieces):
        wob[me, k] = wo_ref[:, k * wide : (k + 1) * wide]
    acc[...] = jnp.zeros_like(acc)

    w_wait(zi, oy)
    w_send(zi, oy, wbuf.at[zi, oy])
    sends[0].start()
    m_copy.start()
    h_wait(y, x_t)
    sends[5].start()

    def o_copy(kind, z, k):
        target = (right, left, nbr)[kind]
        piece = wob.at[2 * z + y, k]
        return rcopy(
            piece, piece, osend.at[kind, z, k], orecv.at[2 * z + y, k], target, t
        )

    def o_wait(slot, k):
        piece = wob.at[slot, k]
        rcopy(piece, piece, osend.at[2, 0, k], orecv.at[slot, k], nbr, t).wait_recv()

    def forward(s):
        lo = zi - s
        hi = zi + s

        for p in range(2):

            @pl.when(lo >= 0)
            def _():
                w_wait(lo, p)

                @pl.when(has_right)
                def _():
                    w_copy(0, lo, p, wbuf.at[lo, p]).start()

            @pl.when(hi < nz)
            def _():
                w_wait(hi, p)

                @pl.when(has_left)
                def _():
                    w_copy(1, hi, p, wbuf.at[hi, p]).start()

    tile = 256

    def multiply(slot):
        for p in range(2):
            first = (slot * 2 + p) * rows
            block = first // cw
            off = pl.multiple_of(lax.rem(first, cw), 128)

            def step(i, carry):
                b = i // (length // tile)
                r = pl.multiple_of(lax.rem(i, length // tile) * tile, tile)
                acc[b, pl.ds(r, tile), :] += jnp.dot(
                    hidb[b, block, pl.ds(r, tile), pl.ds(off, rows)],
                    wbuf[slot, p],
                    preferred_element_type=jnp.float32,
                )
                return carry

            lax.fori_loop(0, 2 * (length // tile), step, 0)

    def multiply_pair(s):
        @pl.when(zi - s >= 0)
        def _():
            multiply(zi - s)

        @pl.when(zi + s < nz)
        def _():
            multiply(zi + s)

    forward(1)

    for k in range(pieces):

        @pl.when(has_right)
        def _():
            o_copy(0, zi, k).start()

        @pl.when(has_left)
        def _():
            o_copy(1, zi, k).start()

    h_wait(oy, t)
    sends[3].start()
    sends[4].start()
    for k in range(pieces):
        o_copy(2, zi, k).start()

    ones = jnp.ones((8, cw), jnp.bfloat16)

    def row_sums(x):
        x = x.astype(jnp.float32)
        square = x * x
        high = square.astype(jnp.bfloat16)
        low = (square - high.astype(jnp.float32)).astype(jnp.bfloat16)
        return lax.dot_general(
            ones, high, NT_DIMS, preferred_element_type=jnp.float32
        ) + lax.dot_general(ones, low, NT_DIMS, preferred_element_type=jnp.float32)

    def over_tensor(d, src, dst, ss, rs):
        return rcopy(
            src, dst.at[d - 1], ss.at[d - 1], rs.at[d - 1], me, lax.rem(t + d, nt)
        )

    q_load.wait()
    count = qbuf.shape[0]

    def query_norm(i, carry):
        r = pl.multiple_of(i * 128, 128)
        qown[:, pl.ds(r, 128)] = row_sums(qbuf[pl.ds(r, 128), :])
        return carry

    lax.fori_loop(0, count // 128, query_norm, 0)
    q_copies = [over_tensor(d, qown, qrec, qsend, qrecv) for d in range(1, nt)]
    h_wait(oy, x_t)
    sends[6].start()
    for copy in q_copies:
        copy.start()
    if nz > 2:
        forward(2)
    for a, b in ((y, core_t), (oy, core_t)):
        h_wait(a, b)
    x_core = lax.rem(core_t + 2, nt)
    for a, b in ((y, x_core), (oy, x_core)):
        h_wait(a, b)
    for copy in sends:
        copy.wait_send()

    norm_rows = 64

    def normalise(i, carry):
        b = i // (length // norm_rows)
        r = pl.multiple_of(lax.rem(i, length // norm_rows) * norm_rows, norm_rows)
        total = jnp.zeros((norm_rows, 1), jnp.float32)
        for k in range(nt):
            x = hidb[b, k, pl.ds(r, norm_rows), :].astype(jnp.float32)
            total += jnp.sum(x * x, axis=-1, keepdims=True)
        factor = lax.rsqrt(total / d_model + EPS)
        for k in range(nt):
            x = hidb[b, k, pl.ds(r, norm_rows), :].astype(jnp.float32)
            g = gain_ref[k * cw : (k + 1) * cw].astype(jnp.float32)[None, :]
            hidb[b, k, pl.ds(r, norm_rows), :] = (x * factor * g).astype(jnp.bfloat16)
        return carry

    lax.fori_loop(0, 2 * (length // norm_rows), normalise, 0)

    multiply(zi)

    if nz > 2:
        multiply_pair(1)

    def o_forward(s, k):
        lo = zi - s
        hi = zi + s

        @pl.when(lo >= 0)
        def _():
            o_wait(2 * lo + y, k)

            @pl.when(has_right)
            def _():
                o_copy(0, lo, k).start()

            o_copy(2, lo, k).start()

        @pl.when(hi < nz)
        def _():
            o_wait(2 * hi + y, k)

            @pl.when(has_left)
            def _():
                o_copy(1, hi, k).start()

            o_copy(2, hi, k).start()

    early = max(nz - 3, 0)

    def later(s, carry):
        def relay(k, inner):
            o_forward(s - 2, k)
            return inner

        lax.fori_loop(0, pieces, relay, 0)
        forward(s)
        multiply_pair(s - 1)
        return carry

    lax.fori_loop(3, nz, later, 0)
    multiply_pair(nz - 1)
    m_copy.wait()

    def rotate(x):
        return (x * cos_ref[...] + pltpu.roll(x, HEAD // 2, 1) * sin_ref[...]).astype(
            jnp.bfloat16
        )

    def attend(b, out):
        key = rotate(acc[b, :, half_q : half_q + HEAD])
        val = acc[b, :, half_q + HEAD : half_q + 2 * HEAD].T.astype(jnp.bfloat16)
        keep = jnp.broadcast_to(maskb[b].astype(jnp.float32), (128, length)).T[:, 0:1] > 0.5
        for j in range(heads):
            qr = rotate(acc[b, :, j * HEAD : (j + 1) * HEAD])
            logits = lax.dot_general(key, qr, NT_DIMS, preferred_element_type=jnp.float32)
            logits = jnp.where(keep, logits * HEAD**-0.5, -1e30)
            e = jnp.exp(logits - jnp.max(logits, axis=0, keepdims=True))
            w = (e * (1.0 / jnp.sum(e, axis=0, keepdims=True))).astype(jnp.bfloat16)
            o = jnp.dot(val, w, preferred_element_type=jnp.float32)
            out[:, j * HEAD : (j + 1) * HEAD] = o.T.astype(jnp.bfloat16)

    attend(oy, atts)
    a_copy = rcopy(atts, att.at[y], asem.at[0], asem.at[1], nbr, t)
    a_copy.start()
    attend(y, att.at[y])
    a_copy.wait()

    def r_copy(c, k):
        owner = c // nb
        d = lax.rem(owner - t + nt, nt)
        return rcopy(
            rss.at[c, k], rsr.at[d - 1, lax.rem(c, nb), k], rsend.at[c, k],
            rrecv.at[d - 1, lax.rem(c, nb), k], me, owner,
        )

    def project(c, k):
        mine = c // nb == t
        term = jnp.dot(
            att[0], wob[c, k, 0:half_q, :], preferred_element_type=jnp.float32
        ) + jnp.dot(
            att[1], wob[c, k, half_q : 2 * half_q, :], preferred_element_type=jnp.float32
        )

        @pl.when(mine)
        def _():
            hsum[lax.rem(c, nb), k] = term

        @pl.when(jnp.logical_not(mine))
        def _():
            rss[c, k] = term.astype(jnp.bfloat16)
            r_copy(c, k).start()

    def other(z, k):
        @pl.when((z >= 0) & (z < nz))
        def _():
            o_wait(2 * z + oy, k)
            project(2 * z + oy, k)

    def first(k, carry):
        project(me, k)
        other(zi, k)
        return carry

    lax.fori_loop(0, pieces, first, 0)

    def project_pair(s, k):
        @pl.when(zi - s >= 0)
        def _():
            project(2 * (zi - s) + y, k)

        @pl.when(zi + s < nz)
        def _():
            project(2 * (zi + s) + y, k)

    def arrived(i, carry):
        s = 1 + i // pieces
        k = lax.rem(i, pieces)
        project_pair(s, k)
        other(zi - s, k)
        other(zi + s, k)
        return carry

    lax.fori_loop(0, early * pieces, arrived, 0)

    def o_step(i, carry):
        s = 1 + i // pieces
        k = lax.rem(i, pieces)
        o_forward(s, k)
        project_pair(s, k)

        @pl.when(i > early * pieces)
        def _():
            before = 1 + (i - 1) // pieces
            other(zi - before, lax.rem(i - 1, pieces))
            other(zi + before, lax.rem(i - 1, pieces))

        return carry

    lax.fori_loop(early * pieces, (nz - 1) * pieces, o_step, 0)
    other(zi - nz + 1, pieces - 1)
    other(zi + nz - 1, pieces - 1)

    for cb in range(nb):
        for k in range(pieces):
            for d in range(1, nt):
                rcopy(
                    rss.at[0, k], rsr.at[d - 1, cb, k], rsend.at[0, k],
                    rrecv.at[d - 1, cb, k], me, lax.rem(t + d, nt),
                ).wait_recv()

    def add_terms(i, carry):
        r = pl.multiple_of(i * 128, 128)
        part = pl.ds(r, 128)
        for j in range(nb * pieces):
            cols = slice(j * wide, (j + 1) * wide)
            total = hsum[j // pieces, j % pieces, part, :]
            for d in range(1, nt):
                total += rsr[d - 1, j // pieces, j % pieces, part, :].astype(jnp.float32)
            hbuf[part, cols] = (hid_ref[part, cols].astype(jnp.float32) + total).astype(
                jnp.bfloat16
            )
        fown[:, part] = row_sums(hbuf[part, :])
        return carry

    lax.fori_loop(0, length // 128, add_terms, 0)
    f_copies = [over_tensor(d, fown, frec, fsend, frecv) for d in range(1, nt)]
    for copy in f_copies:
        copy.start()
    mask_row = mask_ref[...].astype(jnp.float32)
    tokens = jnp.sum(mask_row, axis=1, keepdims=True)
    mask_rows = jnp.broadcast_to(mask_row, (8, length)).astype(jnp.bfloat16)
    for copy in f_copies:
        copy.wait_recv()
    squares = fown[0:1, :]
    for d in range(1, nt):
        squares += frec[d - 1][0:1, :]
    factor_row = lax.rsqrt(squares / d_model + EPS)
    colb[...] = jnp.broadcast_to(factor_row, (128, length)).T

    def final_norm(i, carry):
        r = pl.multiple_of(i * norm_rows, norm_rows)
        part = pl.ds(r, norm_rows)
        x = hbuf[part, :].astype(jnp.float32)
        g = fgain_ref[...].astype(jnp.float32)[None, :]
        hbuf[part, :] = (x * colb[part, 0:1] * g).astype(jnp.bfloat16)
        return carry

    lax.fori_loop(0, length // norm_rows, final_norm, 0)

    for j in range(cw // HEAD):
        cols = slice(j * HEAD, (j + 1) * HEAD)
        hn = hbuf[:, cols]
        lat = lat_ref[:, cols]
        logits = lax.dot_general(lat, hn, NT_DIMS, preferred_element_type=jnp.float32)
        logits = logits * HEAD**-0.5
        e = jnp.exp(logits - jnp.max(logits, axis=0, keepdims=True))
        w = (e * (1.0 / jnp.sum(e, axis=0, keepdims=True))).astype(jnp.bfloat16)
        seen = lax.dot_general(mask_rows, w, NT_DIMS, preferred_element_type=jnp.float32)
        high = seen.astype(jnp.bfloat16)
        low = (seen - high.astype(jnp.float32)).astype(jnp.bfloat16)
        total = (
            jnp.dot(mask_rows, hn, preferred_element_type=jnp.float32)
            + jnp.dot(high, lat, preferred_element_type=jnp.float32)
            + jnp.dot(low, lat, preferred_element_type=jnp.float32)
        )
        prow[me, :, cols] = total / tokens

    def p_copy(d):
        return rcopy(
            prow.at[me], prow.at[me], psend.at[d - 1], precv.at[me], lax.rem(me + d, ndp), t
        )

    def p_start(d, carry):
        p_copy(d).start()
        return carry

    def p_wait(d, carry):
        src = lax.rem(me + d, ndp)
        rcopy(
            prow.at[src], prow.at[src], psend.at[d - 1], precv.at[src], src, t
        ).wait_recv()
        return carry

    lax.fori_loop(1, ndp, p_start, 0)
    lax.fori_loop(1, ndp, p_wait, 0)
    every = jnp.concatenate([prow[i, 0:1, :] for i in range(ndp)], axis=0)
    sown[:, count:] = jnp.broadcast_to(
        jnp.sum(every * every, axis=1, keepdims=True), (ndp, 128)
    )
    every = every.astype(jnp.bfloat16)

    def score(i, carry):
        r = pl.multiple_of(i * 256, 256)
        sown[:, pl.ds(r, 256)] = lax.dot_general(
            every, qbuf[pl.ds(r, 256), :], NT_DIMS, preferred_element_type=jnp.float32
        )
        return carry

    lax.fori_loop(0, count // 256, score, 0)
    s_copies = [over_tensor(d, sown, srec, ssend, srecv) for d in range(1, nt)]
    for copy in s_copies:
        copy.start()
    for copy in q_copies + s_copies:
        copy.wait_recv()
    scores = sown[...]
    query_sq = qown[0:1, :]
    for d in range(1, nt):
        scores += srec[d - 1]
        query_sq += qrec[d - 1][0:1, :]
    similarity = (
        scores[:, :count]
        * lax.rsqrt(scores[:, count : count + 1] + 1e-06)
        * (lax.rsqrt(query_sq + 1e-06) / logit_divisor)
    )
    sim_ref[...] = similarity
    top = jnp.max(similarity, axis=0, keepdims=True)
    norm_ref[...] = top + jnp.log(jnp.sum(jnp.exp(similarity - top), axis=0, keepdims=True))

    for copy in f_copies + q_copies + s_copies:
        copy.wait_send()

    def p_drain(d, carry):
        p_copy(d).wait_send()
        return carry

    lax.fori_loop(1, ndp, p_drain, 0)

    y_copy.wait_send()

    def drain(z, carry):
        for k in range(pieces):
            o_copy(2, z, k).wait_send()

        @pl.when(has_right & (z <= zi))
        def _():
            for k in range(pieces):
                o_copy(0, z, k).wait_send()
            for p in range(2):
                w_copy(0, z, p, wbuf.at[z, p]).wait_send()

        @pl.when(has_left & (z >= zi))
        def _():
            for k in range(pieces):
                o_copy(1, z, k).wait_send()
            for p in range(2):
                w_copy(1, z, p, wbuf.at[z, p]).wait_send()

        return carry

    lax.fori_loop(0, nz, drain, 0)

    def drain_terms(c, carry):
        @pl.when(c // nb != t)
        def _():
            for k in range(pieces):
                r_copy(c, k).wait_send()

        return carry

    lax.fori_loop(0, ndp, drain_terms, 0)


def layer(ndp, nt, rows, mask, wq, wk, wv, wo, gain, cosine, sine, fgain, lat, queries):
    length, cw = rows.shape
    depth = wq.shape[0]
    pack = (wq.shape[1] + wk.shape[1] + wv.shape[1]) // 2
    half_q = wo.shape[0] // 2
    nz, nb = ndp // 2, ndp // nt
    wide = 128
    pieces = wo.shape[1] // wide
    count = queries.shape[0]
    dma = pltpu.SemaphoreType.DMA
    bf, f32 = jnp.bfloat16, jnp.float32
    vmem = pl.BlockSpec(memory_space=pltpu.VMEM)
    return pl.pallas_call(
        functools.partial(layer_kernel, ndp, nt),
        out_shape=(
            jax.ShapeDtypeStruct((ndp, count), f32),
            jax.ShapeDtypeStruct((1, count), f32),
        ),
        in_specs=[vmem] * 11 + [pl.BlockSpec(memory_space=pl.ANY)],
        out_specs=(vmem, vmem),
        scratch_shapes=[
            pltpu.VMEM((2, nt, length, cw), bf),
            pltpu.VMEM((2,) + mask.shape, mask.dtype),
            pltpu.VMEM((2, depth, pack), bf),
            pltpu.VMEM((nz, 2, depth, pack), bf),
            pltpu.VMEM((ndp, pieces, wo.shape[0], wide), bf),
            pltpu.VMEM((2, length, pack), f32),
            pltpu.VMEM((length, half_q), bf),
            pltpu.VMEM((2, length, half_q), bf),
            pltpu.VMEM((ndp, pieces, length, wide), bf),
            pltpu.VMEM((nt - 1, nb, pieces, length, wide), bf),
            pltpu.VMEM((nb, pieces, length, wide), f32),
            pltpu.VMEM((length, cw), bf),
            pltpu.VMEM((length, 128), f32),
            pltpu.VMEM((8, length), f32),
            pltpu.VMEM((nt - 1, 8, length), f32),
            pltpu.VMEM((count, cw), bf),
            pltpu.VMEM((8, count), f32),
            pltpu.VMEM((nt - 1, 8, count), f32),
            pltpu.VMEM((ndp, 8, cw), f32),
            pltpu.VMEM((ndp, count + 128), f32),
            pltpu.VMEM((nt - 1, ndp, count + 128), f32),
            dma((7,)),
            dma((2, nt)),
            dma((2,)),
            dma,
            dma((2, nz, 2)),
            dma((nz, 2)),
            dma((2,)),
            dma((3, nz, pieces)),
            dma((ndp, pieces)),
            dma((ndp, pieces)),
            dma((nt - 1, nb, pieces)),
            dma((nt - 1,)),
            dma((nt - 1,)),
            dma,
            dma((nt - 1,)),
            dma((nt - 1,)),
            dma((ndp - 1,)),
            dma((ndp,)),
            dma((nt - 1,)),
            dma((nt - 1,)),
        ],
        compiler_params=pltpu.CompilerParams(
            collective_id=0, has_side_effects=True, vmem_limit_bytes=60 * 1024 * 1024
        ),
    )(rows, mask, wq, wk, wv, wo, gain, cosine, sine, fgain, lat, queries)


def local(
    ndp, nt,
    hidden_in, norm_gain, w_query, w_key, w_value, w_out, final_gain, latents, token_mask, queries,
):
    _, length, part_width = hidden_in.shape
    rows = hidden_in.reshape(length, part_width)
    half = HEAD // 2
    freqs = np.float32(10000.0) ** (-2.0 * np.arange(half, dtype=np.float32) / HEAD)
    angle = np.arange(length, dtype=np.float32)[:, None] * freqs.astype(np.float32)[None, :]
    cosine = jnp.asarray(np.concatenate([np.cos(angle)] * 2, axis=1), jnp.float32)
    sine = jnp.asarray(np.concatenate([-np.sin(angle), np.sin(angle)], axis=1), jnp.float32)
    similarity, log_norm = layer(
        ndp, nt, rows, token_mask, w_query, w_key, w_value, w_out, norm_gain, cosine, sine, final_gain,
        latents, queries,
    )
    return similarity.T, log_norm[0]


def solution(mesh):
    placed = (
        P("dp", None, "tensor"),
        P(),
        P("dp", "tensor"),
        P("dp", "tensor"),
        P("dp", "tensor"),
        P("tensor", "dp"),
        P("tensor"),
        P(None, "tensor"),
        P("dp", None),
        P("dp", "tensor"),
    )
    return jax.shard_map(
        functools.partial(local, mesh.shape["dp"], mesh.shape["tensor"]),
        mesh=mesh, in_specs=placed, out_specs=(P("dp", None), P("dp")), check_vma=False,
    )
```
